512 devices in a mesh: row: 32 (over y, z_lo), col: 16 (over x, z_hi, core).
Axes of the slice: x: 4, y: 8, z: 8 (z_hi: 2, z_lo: 4; z = z_hi * 4 + z_lo), core: 2. Of those that a mesh axis runs over, the one named last changes fastest.
Arguments:
- occ_orbitals: bfloat16 [8192, 2048], P(('row', 'col')), may hold values from -2 to 2
- vir_orbitals: bfloat16 [8192, 1024], P(('row', 'col')), may hold values from -2.5 to 2.5
- occ_energy: float32 [2048], replicated, may hold values from -2 to -0.1
- vir_energy: float32 [1024], replicated, may hold values from 0.1 to 2.5
- tau_points: float32 [2], replicated, may hold values from 0.3 to 1.5
Outputs:
- chi0: float32 [2, 8192, 8192], P(None, 'row', 'col')
The draws below stay inside these ranges and needn't reach their ends.
All inputs are finite; a program needn't handle non-finite values.
Results may differ from the reference program's by a relative error of at most 0.00047.
Values may be sent and summed in bfloat16 or wider, within the bound.
A program may use at most 64 MiB of HBM per device.

```python
import jax
import jax.numpy as jnp
from jax import lax

NOCC = 2048
NVIR = 1024
NTAU = 2
P_SIZE = 8192


def block_levels(own_key, dims, shards, low, high):
    def one(axis_at, parts):
        steps = jax.random.uniform(jax.random.fold_in(jax.random.fold_in(own_key, 6), axis_at), (parts,), jnp.float32, low / len(shards), high / len(shards))
        return jnp.repeat(jnp.exp(steps), dims[axis_at] // parts).reshape((-1,) + (1,) * (len(dims) - axis_at - 1))

    factor_of = one(*shards[0])
    for cut in shards[1:]:
        factor_of = factor_of * one(*cut)
    return factor_of


def scatter_about(rng, dims, width, reach, pieces=(), kind=jnp.bfloat16):
    entries = jax.random.normal(rng, dims, jnp.float32) * width
    if len(pieces) > 0:
        entries = block_levels(rng, dims, pieces, -0.22, 0.18) * entries
    return jnp.clip(entries, min=-reach, max=reach).astype(kind)


def setup_inputs(seed: int = 0) -> dict:
    keys = jax.random.split(jax.random.key(seed), 6)
    occ_orbitals = scatter_about(keys[0], (P_SIZE, NOCC), (NOCC ** -0.25), 2.0, ((0, 512),))
    vir_orbitals = scatter_about(keys[1], (P_SIZE, NVIR), (NVIR ** -0.25), 2.5, ((0, 512),))
    occ_energy = jnp.clip(jax.random.uniform(keys[2], (NOCC,), jnp.float32, -2.0, -0.1), -2.0, -0.1)
    vir_energy = jnp.clip(jax.random.uniform(keys[3], (NVIR,), jnp.float32, 0.1, 2.5), 0.1, 2.5)
    tau_points = jnp.clip(jax.random.uniform(keys[4], (NTAU,), jnp.float32, 0.3, 1.5), 0.3, 1.5)
    return dict(occ_orbitals=occ_orbitals, vir_orbitals=vir_orbitals, occ_energy=occ_energy, vir_energy=vir_energy, tau_points=tau_points)


def reference(occ_orbitals, vir_orbitals, occ_energy, vir_energy, tau_points):
    def one_time(tau_value):
        occ_weighted = (occ_orbitals.astype(jnp.float32) * jnp.exp(tau_value * occ_energy)[None, :]).astype(jnp.bfloat16)
        vir_weighted = (vir_orbitals.astype(jnp.float32) * jnp.exp(-tau_value * vir_energy)[None, :]).astype(jnp.bfloat16)
        gram_occ = jnp.dot(occ_weighted, occ_orbitals.T, preferred_element_type=jnp.float32)
        gram_vir = jnp.dot(vir_weighted, vir_orbitals.T, preferred_element_type=jnp.float32)
        return -(gram_occ * gram_vir)

    return lax.map(one_time, tau_points)
```

```python
import jax
import jax.numpy as jnp
from jax import lax
from jax.experimental import pallas as pl
from jax.experimental.pallas import tpu as pltpu
from jax.sharding import PartitionSpec as P

PIECES = 8
OCC_W = 256
VIR_W = 128
WIDTH = OCC_W + VIR_W
BLOCK = 16
ROWS = 256
COLS = 512
GROUP = 4
CHUNK = COLS // GROUP
NTAU = 2
MESH = pl.DeviceIdType.MESH


def gather_and_multiply(
    occ_ref, vir_ref, occ_energy_ref, vir_energy_ref, tau_ref, out_ref,
    own, rows, cols, scales, total_occ, total_vir,
    land_send, land_recv, near_send, near_recv, up_send, up_recv, down_send, down_recv,
    row_send, row_recv, core_send, core_recv, own_sem,
):
    row, col = lax.axis_index("row"), lax.axis_index("col")
    y, g = row // GROUP, row % GROUP

    flip = (g, g + 1 - 2 * (g % 2), (g + 2) % GROUP, GROUP - 1 - g)
    over = col + 2 - 4 * (col // 2 % 2)

    def near(k):
        return (y * GROUP + flip[k], col)

    above = ((row + GROUP) % (PIECES * GROUP), col)
    below = ((row + (PIECES - 1) * GROUP) % (PIECES * GROUP), col)
    across = (row, over)
    sibling = (row, col + 1 - 2 * (col % 2))

    def beside(k):
        return (row, (col + 4 * k) % 16)

    land_g = (row % 2) * 2 + col // 8
    land_col = row // 2
    source_row = 2 * col + g // 2

    def landing(j):
        return j * GROUP + land_g, land_col

    def source(i):
        return source_row, (g % 2) * 8 + i

    def same(place):
        return jnp.logical_and(place[0] == row, place[1] == col)

    barrier = pltpu.get_barrier_semaphore()
    partners = [near(1), near(2), near(3), above, below, across, sibling, beside(1), beside(2), beside(3)]
    partners += [source(i) for i in range(8)]
    for place in partners:
        pl.semaphore_signal(barrier, inc=1, device_id=place, device_id_type=MESH)
    for j in range(PIECES):
        own[j, :, :OCC_W] = occ_ref[:, j * OCC_W:(j + 1) * OCC_W]
        own[j, :, OCC_W:] = vir_ref[:, j * VIR_W:(j + 1) * VIR_W]
        for t in range(NTAU):
            scales[j, t:t + 1, :OCC_W] = jnp.exp(tau_ref[t] * occ_energy_ref[:, j * OCC_W:(j + 1) * OCC_W])
            scales[j, t:t + 1, OCC_W:] = jnp.exp(-tau_ref[t] * vir_energy_ref[:, j * VIR_W:(j + 1) * VIR_W])

    pl.semaphore_wait(barrier, len(partners))

    def remote(src, dst, send, recv, place):
        return pltpu.make_async_remote_copy(
            src_ref=src, dst_ref=dst, send_sem=send, recv_sem=recv, device_id=place, device_id_type=MESH
        )

    def land_copy(j):
        spot = cols.at[j, pl.ds(pl.multiple_of(land_g * CHUNK + (col % 8) * BLOCK, BLOCK), BLOCK)]
        return remote(own.at[j], spot, land_send.at[j], land_recv, landing(j))

    for j in range(PIECES):
        @pl.when(same(landing(j)))
        def _():
            spot = cols.at[j, pl.ds(pl.multiple_of(land_g * CHUNK + (col % 8) * BLOCK, BLOCK), BLOCK)]
            pltpu.make_async_copy(own.at[j], spot, land_recv).start()

        @pl.when(jnp.logical_not(same(landing(j))))
        def _():
            land_copy(j).start()

    def row_spot(c):
        return rows.at[:, pl.ds(pl.multiple_of(c * BLOCK, BLOCK), BLOCK)]

    def row_copy(which, k):
        src = own if which == 0 else row_spot(over)
        c = col if which == 0 else over
        place = across if k == 0 else beside(k)
        return remote(src, row_spot(c), row_send.at[which, k], row_recv.at[which, k], place)

    def row_arrival(which, k):
        c = over if k == 0 else ((over if which else col) + 16 - 4 * k) % 16
        return c, remote(row_spot(c), row_spot(c), row_send.at[which, k], row_recv.at[which, k], sibling)

    def core_copy(slot, c, src=None):
        return remote(row_spot(c) if src is None else src, row_spot(c), core_send.at[slot], core_recv.at[slot], sibling)

    own_copy = pltpu.make_async_copy(own, row_spot(col), own_sem)
    own_copy.start()
    row_copies = [row_copy(0, k) for k in range(4)]
    core_copies = [core_copy(0, col, own)]
    for copy in row_copies + core_copies:
        copy.start()

    def chunk(j, k):
        return cols.at[j, pl.ds(pl.multiple_of(flip[k] * CHUNK, CHUNK), CHUNK)]

    def up_copy(step, k):
        j = (y + PIECES - step) % PIECES
        return remote(chunk(j, k), chunk(j, k), up_send.at[step, k], up_recv.at[step, k], above)

    def down_copy(step, k):
        j = (y + step) % PIECES
        return remote(chunk(j, k), chunk(j, k), down_send.at[step, k], down_recv.at[step, k], below)

    def up_wait(step, k):
        j = (y + PIECES - step - 1) % PIECES
        remote(chunk(j, k), chunk(j, k), up_send.at[step, k], up_recv.at[step, k], above).wait_recv()

    def down_wait(step, k):
        j = (y + step + 1) % PIECES
        remote(chunk(j, k), chunk(j, k), down_send.at[step, k], down_recv.at[step, k], below).wait_recv()

    ring_copies = []

    def forward(step, k, up, down):
        if up:
            ring_copies.append(up_copy(step, k))
            ring_copies[-1].start()
        if down:
            ring_copies.append(down_copy(step, k))
            ring_copies[-1].start()

    pltpu.make_async_copy(chunk(y, 0), chunk(y, 0), land_recv).wait()
    near_copies = [remote(chunk(y, 0), chunk(y, 0), near_send.at[k], near_recv.at[k], near(k)) for k in range(1, 4)]
    forward(0, 0, True, True)
    for copy in near_copies:
        copy.start()
    for k in range(1, 4):
        remote(chunk(y, k), chunk(y, k), near_send.at[k], near_recv.at[k], near(k)).wait_recv()
        forward(0, k, True, True)

    c, arrival = row_arrival(0, 0)
    arrival.wait_recv()
    second = [row_copy(1, k) for k in range(1, 4)] + [core_copy(1, c)]
    for copy in second:
        copy.start()
    row_copies += second[:3]
    core_copies.append(second[3])

    for k in range(GROUP):
        up_wait(0, k)
        forward(1, k, True, False)
        down_wait(0, k)
        forward(1, k, False, True)

    slot = 2
    for which in range(2):
        for k in (1, 3, 2):
            c, arrival = row_arrival(which, k)
            arrival.wait_recv()
            core_copies.append(core_copy(slot, c))
            core_copies[-1].start()
            slot += 1

    own_copy.wait()
    for at in range(8):
        core_copies[at].wait_recv()

    contract = (((1,), (1,)), ((), ()))

    def grams(j, t):
        panel = rows[j].astype(jnp.float32)
        weighted = (panel * scales[j, pl.ds(t, 1), :]).astype(jnp.bfloat16)
        gram_occ = lax.dot_general(
            weighted[:, :OCC_W], cols[j, :, :OCC_W], contract, preferred_element_type=jnp.float32
        )
        gram_vir = lax.dot_general(
            weighted[:, OCC_W:], cols[j, :, OCC_W:], contract, preferred_element_type=jnp.float32
        )
        return gram_occ, gram_vir

    def accumulate(j, first=False):
        @pl.loop(0, NTAU)
        def _(t):
            gram_occ, gram_vir = grams(j, t)
            if first:
                total_occ[t] = gram_occ
                total_vir[t] = gram_vir
            else:
                total_occ[t] += gram_occ
                total_vir[t] += gram_vir

    accumulate(y, True)
    accumulate((y + 7) % PIECES)
    accumulate((y + 1) % PIECES)

    for step in (1, 2):
        for k in range(GROUP):
            up_wait(step, k)
            forward(step + 1, k, step < 2 or k < 2, False)
            down_wait(step, k)
            forward(step + 1, k, False, step < 2 or k >= 2)
        accumulate((y + 7 - step) % PIECES)
        accumulate((y + 1 + step) % PIECES)

    for k in range(2):
        up_wait(3, k)
        down_wait(3, k + 2)

    last = (y + 4) % PIECES
    for t in range(NTAU):
        gram_occ, gram_vir = grams(last, t)
        out_ref[t] = -((total_occ[t] + gram_occ) * (total_vir[t] + gram_vir))

    for copy in ring_copies + near_copies + row_copies + core_copies:
        copy.wait_send()
    for j in range(PIECES):
        @pl.when(jnp.logical_not(same(landing(j))))
        def _():
            land_copy(j).wait_send()


def local(occ_orbitals, vir_orbitals, occ_energy, vir_energy, tau_points):
    dma = pltpu.SemaphoreType.DMA
    vmem = pl.BlockSpec(memory_space=pltpu.VMEM)
    return pl.pallas_call(
        gather_and_multiply,
        out_shape=jax.ShapeDtypeStruct((NTAU, ROWS, COLS), jnp.float32),
        in_specs=[vmem, vmem, vmem, vmem, pl.BlockSpec(memory_space=pltpu.SMEM)],
        out_specs=vmem,
        scratch_shapes=[
            pltpu.VMEM((PIECES, BLOCK, WIDTH), jnp.bfloat16),
            pltpu.VMEM((PIECES, ROWS, WIDTH), jnp.bfloat16),
            pltpu.VMEM((PIECES, COLS, WIDTH), jnp.bfloat16),
            pltpu.VMEM((PIECES, NTAU, WIDTH), jnp.float32),
            pltpu.VMEM((NTAU, ROWS, COLS), jnp.float32),
            pltpu.VMEM((NTAU, ROWS, COLS), jnp.float32),
            dma((PIECES,)), dma,
            dma((GROUP,)), dma((GROUP,)),
            dma((4, GROUP)), dma((4, GROUP)),
            dma((4, GROUP)), dma((4, GROUP)),
            dma((2, 4)), dma((2, 4)),
            dma((8,)), dma((8,)),
            dma,
        ],
        compiler_params=pltpu.CompilerParams(
            collective_id=0, has_side_effects=True, vmem_limit_bytes=48 * 2**20
        ),
        cost_estimate=pl.CostEstimate(flops=1610612736, bytes_accessed=2**21, transcendentals=6144),
    )(occ_orbitals, vir_orbitals, occ_energy.reshape(1, -1), vir_energy.reshape(1, -1), tau_points)


def solution(mesh):
    placed = (P(("row", "col"), None), P(("row", "col"), None), P(), P(), P())
    return jax.shard_map(
        local, mesh=mesh, in_specs=placed, out_specs=P(None, "row", "col"), check_vma=False
    )
```

```python
import jax
import jax.numpy as jnp
from jax import lax
from jax.experimental import pallas as pl
from jax.experimental.pallas import tpu as pltpu
from jax.sharding import PartitionSpec as P

SLICES = 8
OCC_W = 256
VIR_W = 128
WIDTH = OCC_W + VIR_W
BLOCK = 16
ROWS = 256
COLS = 512
RUN = 4
NTAU = 2
CARRIED = (0, 2, 3)
MESH = pl.DeviceIdType.MESH


def gather_and_multiply(
    occ_hbm, vir_hbm, occ_energy_hbm, vir_energy_hbm, tau_hbm, out_ref,
    occ, vir, occ_energy, vir_energy, tau, own, scattered, lined, rows, cols, scales, total_occ, total_vir,
    in_sem, y_send, y_recv, x_send, x_recv, z_send, z_recv, up_send, up_recv, down_send, down_recv,
    pair_send, pair_recv, row_send, row_recv, core_send, core_recv, own_sem,
):
    row, col = lax.axis_index("row"), lax.axis_index("col")
    y, z_lo = row // RUN, row % RUN
    x, z_hi, core = col // 4, col // 2 % 2, col % 2

    def flip(value, k):
        return (value, value + 1 - 2 * (value % 2), (value + 2) % 4, 3 - value)[k]

    def at_y(steps):
        return ((row + RUN * steps) % (SLICES * RUN), col)

    def at_x(steps):
        return (row, (col + 4 * steps) % 16)

    over = col + 2 - 4 * z_hi
    across = (row, over)
    sibling = (row, col + 1 - 2 * core)
    pair = (y * RUN + flip(z_lo, 1), col)

    part = 2 * z_hi + z_lo % 2

    def spread(half, k):
        return (y * RUN + flip(part, k), 4 * x + 2 * half + z_lo // 2)

    def spread_source(k, source_core):
        chunk_at = flip(z_lo, k)
        return (y * RUN + 2 * core + chunk_at % 2, 4 * x + 2 * (chunk_at // 2) + source_core)

    inputs = [
        pltpu.make_async_copy(src, dst, in_sem.at[i])
        for i, (src, dst) in enumerate((
            (occ_hbm, occ), (vir_hbm, vir), (occ_energy_hbm, occ_energy), (vir_energy_hbm, vir_energy), (tau_hbm, tau),
        ))
    ]
    for copy in inputs:
        copy.start()

    barrier = pltpu.get_barrier_semaphore()
    partners = [at_y(s) for s in (4, 3, 5, 2, 6, 1, 7)] + [across] + [at_x(s) for s in (2, 1, 3)] + [pair, sibling]
    partners += [spread_source(k, c) for k in CARRIED for c in range(2)]
    for place in partners:
        pl.semaphore_signal(barrier, inc=1, device_id=place, device_id_type=MESH)

    inputs[0].wait()
    inputs[1].wait()
    for j in range(SLICES):
        own[j, :, :OCC_W] = occ[:, j * OCC_W:(j + 1) * OCC_W]
        own[j, :, OCC_W:] = vir[:, j * VIR_W:(j + 1) * VIR_W]
    pl.semaphore_wait(barrier, len(partners))

    def remote(src, dst, send, recv, place):
        return pltpu.make_async_remote_copy(
            src_ref=src, dst_ref=dst, send_sem=send, recv_sem=recv, device_id=place, device_id_type=MESH
        )

    sent = []

    def send(*args):
        sent.append(remote(*args))
        sent[-1].start()

    def arrived(ref, sem):
        pltpu.make_async_copy(ref, ref, sem).wait()

    for steps in (1, 7, 2, 6, 3, 5, 4):
        send(own.at[(y + steps) % SLICES], scattered.at[y], y_send.at[steps], y_recv, at_y(steps))
    pltpu.make_async_copy(own.at[y], scattered.at[y], y_recv).start()

    def row_spot(c):
        return rows.at[:, pl.ds(pl.multiple_of(c * BLOCK, BLOCK), BLOCK)]

    send(own, row_spot(col), row_send.at[0, 0], row_recv.at[0, 0], across)
    send(own, row_spot(col), core_send.at[0], core_recv.at[0], sibling)
    own_copy = pltpu.make_async_copy(own, row_spot(col), own_sem)
    own_copy.start()

    for i in range(2, 5):
        inputs[i].wait()
    for j in range(SLICES):
        for t in range(NTAU):
            tau_at = tau[:, t:t + 1]
            scales[j, t:t + 1, :OCC_W] = jnp.exp(tau_at * occ_energy[:, j * OCC_W:(j + 1) * OCC_W])
            scales[j, t:t + 1, OCC_W:] = jnp.exp(-tau_at * vir_energy[:, j * VIR_W:(j + 1) * VIR_W])

    arrived(scattered, y_recv)
    for steps in (1, 3, 2):
        there = (x + steps) % 4
        send(scattered.at[pl.ds(2 * there, 2)], lined.at[:, x], x_send.at[steps], x_recv, at_x(steps))
    pltpu.make_async_copy(scattered.at[pl.ds(2 * x, 2)], lined.at[:, x], x_recv).start()
    for steps in (1, 3, 2):
        send(own, row_spot(col), row_send.at[0, steps], row_recv.at[0, steps], at_x(steps))

    arrived(lined, x_recv)
    spread_copies = []
    for k in CARRIED:
        for half in range(2):
            place = spread(half, k)
            spot = cols.at[y, z_lo % 2, :, z_hi, pl.ds(pl.multiple_of(core * BLOCK, BLOCK), BLOCK)]
            here = jnp.logical_and(place[0] == row, place[1] == col)
            copy = remote(lined.at[half], spot, z_send.at[half, k], z_recv.at[k], place)
            spread_copies.append((here, copy))

            @pl.when(here)
            def _():
                pltpu.make_async_copy(lined.at[half], spot, z_recv.at[k]).start()

            @pl.when(jnp.logical_not(here))
            def _():
                copy.start()

    def chunk(j, k, xs=slice(0, 4)):
        at = flip(z_lo, k)
        return cols.at[j, at % 2, pl.ds(xs.start, xs.stop - xs.start), at // 2]

    whole, first, second = slice(0, 4), slice(0, 2), slice(2, 4)
    last_up = {CARRIED[0]: whole, CARRIED[1]: first}
    last_down = {CARRIED[2]: whole, CARRIED[1]: second}

    def pass_up(step, k, xs=whole):
        ref = chunk((y + SLICES - step) % SLICES, k, xs)
        send(ref, ref, up_send.at[step, k], up_recv.at[step, k], at_y(1))

    def pass_down(step, k, xs=whole):
        ref = chunk((y + step) % SLICES, k, xs)
        send(ref, ref, down_send.at[step, k], down_recv.at[step, k], at_y(7))

    def share(distance, j):
        send(chunk(j, 0), chunk(j, 0), pair_send.at[distance], pair_recv.at[distance], pair)

    def from_spread(k):
        arrived(chunk(y, k), z_recv.at[k])
        pass_up(0, k)
        pass_down(0, k)
        if k == 0:
            share(0, y)

    def from_below(step, k):
        xs = whole if step < 3 else last_up[k]
        j = (y + SLICES - step - 1) % SLICES
        arrived(chunk(j, k, xs), up_recv.at[step, k])
        if step < 2:
            pass_up(step + 1, k)
        elif step == 2 and k in last_up:
            pass_up(3, k, last_up[k])
        if k == 0:
            share(SLICES - step - 1, j)

    def from_above(step, k):
        xs = whole if step < 3 else last_down[k]
        j = (y + step + 1) % SLICES
        arrived(chunk(j, k, xs), down_recv.at[step, k])
        if step < 2:
            pass_down(step + 1, k)
        elif step == 2 and k in last_down:
            pass_down(3, k, last_down[k])
        if k == 0:
            share(step + 1, j)

    contract = (((1,), (1,)), ((), ()))

    def grams(j, t):
        panel = rows[j].astype(jnp.float32)
        weighted = (panel * scales[j, pl.ds(t, 1), :]).astype(jnp.bfloat16)
        columns = cols[j].reshape(COLS, WIDTH)
        gram_occ = lax.dot_general(
            weighted[:, :OCC_W], columns[:, :OCC_W], contract, preferred_element_type=jnp.float32
        )
        gram_vir = lax.dot_general(
            weighted[:, OCC_W:], columns[:, OCC_W:], contract, preferred_element_type=jnp.float32
        )
        return gram_occ, gram_vir

    def accumulate(distance):
        j = (y + distance) % SLICES
        arrived(chunk(j, 1), pair_recv.at[distance])

        @pl.loop(0, NTAU)
        def _(t):
            gram_occ, gram_vir = grams(j, t)
            if distance == 0:
                total_occ[t] = gram_occ
                total_vir[t] = gram_vir
            else:
                total_occ[t] += gram_occ
                total_vir[t] += gram_vir

    def rows_from_across():
        arrived(row_spot(over), row_recv.at[0, 0])
        for steps in (1, 3, 2):
            send(row_spot(over), row_spot(over), row_send.at[1, steps], row_recv.at[1, steps], at_x(steps))
        send(row_spot(over), row_spot(over), core_send.at[1], core_recv.at[1], sibling)

    def rows_from_beside(which):
        for i, steps in enumerate((1, 3, 2)):
            c = ((over if which else col) + 16 - 4 * steps) % 16
            arrived(row_spot(c), row_recv.at[which, steps])
            slot = 2 + 3 * which + i
            send(row_spot(c), row_spot(c), core_send.at[slot], core_recv.at[slot], sibling)

    def rows_complete():
        own_copy.wait()
        for slot in range(8):
            arrived(row_spot(col), core_recv.at[slot])

    events = [(0.0, rows_from_across, ())]
    for i, k in enumerate(CARRIED):
        events.append((2.5 * (i + 1), from_spread, (k,)))
        for step in range(3):
            at = 2.5 * (i + 1) + 4.2 + 6.2 * step
            events += [(at, from_below, (step, k)), (at, from_above, (step, k))]
    events += [(11.0, rows_from_beside, (0,)), (13.0, rows_from_beside, (1,)), (17.0, rows_complete, ())]
    events += [(18.0, accumulate, (0,)), (18.1, accumulate, (1,)), (18.2, accumulate, (7,))]
    events += [(23.0, accumulate, (2,)), (23.1, accumulate, (6,))]
    events += [(40.0, from_below, (3, k)) for k in last_up] + [(41.0, from_above, (3, k)) for k in last_down]
    events += [(42.0, accumulate, (3,)), (42.1, accumulate, (5,))]
    for _, wait_for, args in sorted(events, key=lambda event: event[0]):
        wait_for(*args)

    last = (y + 4) % SLICES
    arrived(chunk(last, 1), pair_recv.at[4])
    for t in range(NTAU):
        gram_occ, gram_vir = grams(last, t)
        out_ref[t] = -((total_occ[t] + gram_occ) * (total_vir[t] + gram_vir))

    for copy in sent:
        copy.wait_send()
    for here, copy in spread_copies:
        @pl.when(jnp.logical_not(here))
        def _():
            copy.wait_send()


def local(occ_orbitals, vir_orbitals, occ_energy, vir_energy, tau_points):
    dma = pltpu.SemaphoreType.DMA
    place = pl.BlockSpec(memory_space=pl.ANY)
    bf16, f32 = jnp.bfloat16, jnp.float32
    return pl.pallas_call(
        gather_and_multiply,
        out_shape=jax.ShapeDtypeStruct((NTAU, ROWS, COLS), f32),
        in_specs=[place] * 5,
        out_specs=pl.BlockSpec(memory_space=pltpu.VMEM),
        scratch_shapes=[
            pltpu.VMEM(occ_orbitals.shape, bf16),
            pltpu.VMEM(vir_orbitals.shape, bf16),
            pltpu.VMEM((1, SLICES * OCC_W), f32),
            pltpu.VMEM((1, SLICES * VIR_W), f32),
            pltpu.VMEM((1, NTAU), f32),
            pltpu.VMEM((SLICES, BLOCK, WIDTH), bf16),
            pltpu.VMEM((SLICES, BLOCK, WIDTH), bf16),
            pltpu.VMEM((2, 4, BLOCK, WIDTH), bf16),
            pltpu.VMEM((SLICES, ROWS, WIDTH), bf16),
            pltpu.VMEM((SLICES, 2, 4, 2, 2 * BLOCK, WIDTH), bf16),
            pltpu.VMEM((SLICES, NTAU, WIDTH), f32),
            pltpu.VMEM((NTAU, ROWS, COLS), f32),
            pltpu.VMEM((NTAU, ROWS, COLS), f32),
            dma((5,)),
            dma((SLICES,)), dma,
            dma((4,)), dma,
            dma((2, 4)), dma((4,)),
            dma((4, 4)), dma((4, 4)),
            dma((4, 4)), dma((4, 4)),
            dma((SLICES,)), dma((SLICES,)),
            dma((2, 4)), dma((2, 4)),
            dma((8,)), dma((8,)),
            dma,
        ],
        compiler_params=pltpu.CompilerParams(
            collective_id=0, has_side_effects=True, vmem_limit_bytes=56 * 2**20
        ),
        cost_estimate=pl.CostEstimate(flops=1610612736, bytes_accessed=2**21, transcendentals=6144),
    )(occ_orbitals, vir_orbitals, occ_energy.reshape(1, -1), vir_energy.reshape(1, -1), tau_points.reshape(1, -1))


def solution(mesh):
    placed = (P(("row", "col"), None), P(("row", "col"), None), P(), P(), P())
    return jax.shard_map(
        local, mesh=mesh, in_specs=placed, out_specs=P(None, "row", "col"), check_vma=False
    )
```

```python
import jax
import jax.numpy as jnp
from jax import lax
from jax.experimental import pallas as pl
from jax.experimental.pallas import tpu as pltpu
from jax.sharding import PartitionSpec as P

SLICES = 8
OCC_W = 256
VIR_W = 128
WIDTH = OCC_W + VIR_W
BLOCK = 16
ROWS = 256
COLS = 512
RUN = 4
NTAU = 2
MESH = pl.DeviceIdType.MESH


def gather_and_multiply(
    occ_hbm, vir_hbm, occ_energy_hbm, vir_energy_hbm, tau_hbm, out_ref,
    occ, vir, occ_energy, vir_energy, tau, own, scattered, lined, rows, cols, scales, total_occ, total_vir,
    in_sem, y_send, y_recv, x_send, x_recv, z_send, z_recv, up_send, up_recv, down_send, down_recv,
    pair_send, pair_recv, row_send, row_recv, core_send, core_recv, own_sem, go,
):
    row, col = lax.axis_index("row"), lax.axis_index("col")
    y, z_lo = row // RUN, row % RUN
    x, z_hi, core = col // 4, col // 2 % 2, col % 2

    def at_y(steps):
        return ((row + RUN * steps) % (SLICES * RUN), col)

    def at_x(steps):
        return (row, (col + 4 * steps) % 16)

    over = col + 2 - 4 * z_hi
    across = (row, over)
    sibling = (row, col + 1 - 2 * core)
    pair = (y * RUN + z_lo + 1 - 2 * (z_lo % 2), col)

    parity, owner = z_lo % 2, z_lo // 2

    def spread(half, to):
        return (y * RUN + to, 4 * x + 2 * half + owner)

    def early_source(source_core):
        return (y * RUN + 2 * core + parity, 4 * x + source_core)

    def late_source(p, source_core):
        return (y * RUN + 2 * core + p, 4 * x + 2 + source_core)

    early, late = z_hi == 0, z_hi == 1

    inputs = [
        pltpu.make_async_copy(src, dst, in_sem.at[i])
        for i, (src, dst) in enumerate((
            (occ_hbm, occ), (vir_hbm, vir), (occ_energy_hbm, occ_energy), (vir_energy_hbm, vir_energy), (tau_hbm, tau),
        ))
    ]
    for copy in inputs:
        copy.start()

    barrier = pltpu.get_barrier_semaphore()
    lates = [late_source(p, c) for p in range(2) for c in range(2)]
    earlies = [early_source(c) for c in range(2)]
    partners = [at_y(s) for s in (4, 3, 5, 2, 6, 1, 7)] + [at_x(s) for s in (2, 1, 3)] + [pair, sibling]

    def signal(semaphore, places):
        for place in places:
            pl.semaphore_signal(semaphore, inc=1, device_id=place, device_id_type=MESH)

    signal(barrier, partners)

    @pl.when(early)
    def _():
        signal(barrier, [across] + lates + earlies + [spread(1, parity + 2 * i) for i in range(2)])

    @pl.when(late)
    def _():
        signal(barrier, lates)

    inputs[0].wait()
    inputs[1].wait()
    for j in range(SLICES):
        own[j, :, :OCC_W] = occ[:, j * OCC_W:(j + 1) * OCC_W]
        own[j, :, OCC_W:] = vir[:, j * VIR_W:(j + 1) * VIR_W]
    pl.semaphore_wait(barrier, len(partners) + 2 + 9 * z_hi)

    @pl.when(late)
    def _():
        signal(go, [across] + earlies)


    def remote(src, dst, send, recv, place):
        return pltpu.make_async_remote_copy(
            src_ref=src, dst_ref=dst, send_sem=send, recv_sem=recv, device_id=place, device_id_type=MESH
        )

    sent = []

    def launch(build, *args):
        sent.append((build, args))
        build(*args).start()

    def send(*args):
        launch(remote, *args)

    def arrived(ref, sem):
        pltpu.make_async_copy(ref, ref, sem).wait()

    for steps in (1, 7, 2, 6, 3, 5, 4):
        send(own.at[(y + steps) % SLICES], scattered.at[y], y_send.at[steps], y_recv, at_y(steps))
    pltpu.make_async_copy(own.at[y], scattered.at[y], y_recv).start()

    def row_spot(c):
        return rows.at[:, pl.ds(pl.multiple_of(c * BLOCK, BLOCK), BLOCK)]

    row_across = remote(own, row_spot(col), row_send.at[0, 0], row_recv.at[0, 0], across)
    sent.append((lambda: row_across, ()))

    @pl.when(late)
    def _():
        row_across.start()

    send(own, row_spot(col), core_send.at[0], core_recv.at[0], sibling)
    own_copy = pltpu.make_async_copy(own, row_spot(col), own_sem)
    own_copy.start()

    for i in range(2, 5):
        inputs[i].wait()
    for j in range(SLICES):
        for t in range(NTAU):
            tau_at = tau[:, t:t + 1]
            scales[j, t:t + 1, :OCC_W] = jnp.exp(tau_at * occ_energy[:, j * OCC_W:(j + 1) * OCC_W])
            scales[j, t:t + 1, OCC_W:] = jnp.exp(-tau_at * vir_energy[:, j * VIR_W:(j + 1) * VIR_W])

    arrived(scattered, y_recv)
    for steps in (1, 3, 2):
        there = (x + steps) % 4
        send(scattered.at[pl.ds(2 * there, 2)], lined.at[:, x], x_send.at[steps], x_recv, at_x(steps))
    pltpu.make_async_copy(scattered.at[pl.ds(2 * x, 2)], lined.at[:, x], x_recv).start()

    arrived(lined, x_recv)
    spread_copies = []

    def spread_out(kind, half, to, active, slot):
        place = spread(half, to)
        spot = cols.at[y, parity, :, z_hi, pl.ds(pl.multiple_of(core * BLOCK, BLOCK), BLOCK)]
        here = jnp.logical_and(place[0] == row, place[1] == col)
        copy = remote(lined.at[half], spot, z_send.at[slot], z_recv.at[kind], place)
        there = jnp.logical_and(active, jnp.logical_not(here))
        spread_copies.append((there, copy))

        @pl.when(jnp.logical_and(active, here))
        def _():
            pltpu.make_async_copy(lined.at[half], spot, z_recv.at[kind]).start()

        @pl.when(there)
        def _():
            copy.start()

    for i in range(2):
        spread_out(0, 0, parity + 2 * i, early, i)
    for to in range(RUN):
        for half in range(2):
            spread_out(1 + parity, half, to, late, 4 + 2 * to + half)

    def to_late_half():
        @pl.when(early)
        def _():
            pl.semaphore_wait(go, 3)

        for i in range(2):
            spread_out(0, 1, parity + 2 * i, early, 2 + i)

    def early_row_across():
        @pl.when(early)
        def _():
            row_across.start()

    def chunk(j, kind, xs=slice(0, 4)):
        p = (parity, 0, 1, 1 - parity)[kind]
        return cols.at[j, p, pl.ds(xs.start, xs.stop - xs.start), (0, 1, 1, 0)[kind]]

    whole, first, second = slice(0, 4), slice(0, 2), slice(2, 4)
    last_up = {0: first, 1: whole}
    last_down = {0: second, 2: whole}

    def up_copy(step, k, xs):
        ref = chunk((y + SLICES - step) % SLICES, k, xs)
        return remote(ref, ref, up_send.at[step, k], up_recv.at[step, k], at_y(1))

    def down_copy(step, k, xs):
        ref = chunk((y + step) % SLICES, k, xs)
        return remote(ref, ref, down_send.at[step, k], down_recv.at[step, k], at_y(7))

    def pair_copy(slot, xs):
        ref = chunk((y + (4 if slot == 8 else slot)) % SLICES, 0, xs)
        return remote(ref, ref, pair_send.at[slot], pair_recv.at[slot], pair)

    def pass_up(step, k, xs=whole):
        launch(up_copy, step, k, xs)

    def pass_down(step, k, xs=whole):
        launch(down_copy, step, k, xs)

    def share(slot, xs=whole):
        launch(pair_copy, slot, xs)

    def from_spread(k):
        arrived(chunk(y, k), z_recv.at[k])
        pass_up(0, k)
        pass_down(0, k)
        if k == 0:
            share(0)

    def from_below(step, k):
        xs = whole if step < 3 else last_up[k]
        j = (y + SLICES - step - 1) % SLICES
        arrived(chunk(j, k, xs), up_recv.at[step, k])
        if step < 2:
            pass_up(step + 1, k)
        elif step == 2 and k in last_up:
            pass_up(3, k, last_up[k])
        if k == 0:
            share(SLICES - step - 1, xs)

    def from_above(step, k):
        xs = whole if step < 3 else last_down[k]
        j = (y + step + 1) % SLICES
        arrived(chunk(j, k, xs), down_recv.at[step, k])
        if step < 2:
            pass_down(step + 1, k)
        elif step == 2 and k in last_down:
            pass_down(3, k, last_down[k])
        if k == 0:
            share(step + 1 if step < 3 else 8, xs)

    def from_both(step, k):
        from_below(step, k)
        from_above(step, k)

    def only(half, step, k):
        count = len(sent)

        @pl.when(half)
        def _():
            from_both(step, k)
        again = sent[count:]
        del sent[count:]
        return again

    contract = (((1,), (1,)), ((), ()))

    def grams(j, t):
        panel = rows[j].astype(jnp.float32)
        weighted = (panel * scales[j, pl.ds(t, 1), :]).astype(jnp.bfloat16)
        columns = cols[j].reshape(COLS, WIDTH)
        gram_occ = lax.dot_general(
            weighted[:, :OCC_W], columns[:, :OCC_W], contract, preferred_element_type=jnp.float32
        )
        gram_vir = lax.dot_general(
            weighted[:, OCC_W:], columns[:, OCC_W:], contract, preferred_element_type=jnp.float32
        )
        return gram_occ, gram_vir

    def accumulate(distance):
        j = (y + distance) % SLICES
        arrived(chunk(j, 3), pair_recv.at[distance])

        @pl.loop(0, NTAU)
        def _(t):
            gram_occ, gram_vir = grams(j, t)
            if distance == 0:
                total_occ[t] = gram_occ
                total_vir[t] = gram_vir
            else:
                total_occ[t] += gram_occ
                total_vir[t] += gram_vir

    def rows_from_across():
        arrived(row_spot(over), row_recv.at[0, 0])
        for steps in (1, 3, 2):
            send(row_spot(over), row_spot(over), row_send.at[1, steps], row_recv.at[1, steps], at_x(steps))
        send(row_spot(over), row_spot(over), core_send.at[1], core_recv.at[1], sibling)

    def rows_from_beside(which):
        for i, steps in enumerate((1, 3, 2)):
            c = ((over if which else col) + 16 - 4 * steps) % 16
            arrived(row_spot(c), row_recv.at[which, steps])
            slot = 2 + 3 * which + i
            send(row_spot(c), row_spot(c), core_send.at[slot], core_recv.at[slot], sibling)

    def rows_complete():
        own_copy.wait()
        for slot in range(8):
            arrived(row_spot(col), core_recv.at[slot])

    to_late_half()
    from_spread(0)
    from_both(0, 0)
    early_row_across()
    sent += only(early, 1, 0)
    from_spread(1)
    for steps in (1, 3, 2):
        send(own, row_spot(col), row_send.at[0, steps], row_recv.at[0, steps], at_x(steps))
    from_spread(2)
    rows_from_across()
    sent += only(early, 2, 0)
    only(late, 1, 0)
    rows_from_beside(0)
    from_both(0, 1)
    from_both(0, 2)
    only(late, 2, 0)
    rows_from_beside(1)
    from_both(1, 1)
    from_both(1, 2)
    rows_complete()
    for distance in (0, 1, 7):
        accumulate(distance)
    from_both(3, 0)
    from_both(2, 1)
    from_both(2, 2)
    for distance in (2, 6, 3, 5):
        accumulate(distance)
    from_below(3, 1)
    from_above(3, 2)

    last = (y + 4) % SLICES
    arrived(chunk(last, 3, first), pair_recv.at[4])
    arrived(chunk(last, 3, second), pair_recv.at[8])
    for t in range(NTAU):
        gram_occ, gram_vir = grams(last, t)
        out_ref[t] = -((total_occ[t] + gram_occ) * (total_vir[t] + gram_vir))

    for build, args in sent:
        build(*args).wait_send()
    for there, copy in spread_copies:
        @pl.when(there)
        def _():
            copy.wait_send()


def local(occ_orbitals, vir_orbitals, occ_energy, vir_energy, tau_points):
    dma = pltpu.SemaphoreType.DMA
    place = pl.BlockSpec(memory_space=pl.ANY)
    bf16, f32 = jnp.bfloat16, jnp.float32
    return pl.pallas_call(
        gather_and_multiply,
        out_shape=jax.ShapeDtypeStruct((NTAU, ROWS, COLS), f32),
        in_specs=[place] * 5,
        out_specs=pl.BlockSpec(memory_space=pltpu.VMEM),
        scratch_shapes=[
            pltpu.VMEM(occ_orbitals.shape, bf16),
            pltpu.VMEM(vir_orbitals.shape, bf16),
            pltpu.VMEM((1, SLICES * OCC_W), f32),
            pltpu.VMEM((1, SLICES * VIR_W), f32),
            pltpu.VMEM((1, NTAU), f32),
            pltpu.VMEM((SLICES, BLOCK, WIDTH), bf16),
            pltpu.VMEM((SLICES, BLOCK, WIDTH), bf16),
            pltpu.VMEM((2, 4, BLOCK, WIDTH), bf16),
            pltpu.VMEM((SLICES, ROWS, WIDTH), bf16),
            pltpu.VMEM((SLICES, 2, 4, 2, 2 * BLOCK, WIDTH), bf16),
            pltpu.VMEM((SLICES, NTAU, WIDTH), f32),
            pltpu.VMEM((NTAU, ROWS, COLS), f32),
            pltpu.VMEM((NTAU, ROWS, COLS), f32),
            dma((5,)),
            dma((SLICES,)), dma,
            dma((4,)), dma,
            dma((12,)), dma((3,)),
            dma((4, 3)), dma((4, 3)),
            dma((4, 3)), dma((4, 3)),
            dma((SLICES + 1,)), dma((SLICES + 1,)),
            dma((2, 4)), dma((2, 4)),
            dma((8,)), dma((8,)),
            dma,
            pltpu.SemaphoreType.REGULAR,
        ],
        compiler_params=pltpu.CompilerParams(
            collective_id=0, has_side_effects=True, vmem_limit_bytes=56 * 2**20
        ),
        cost_estimate=pl.CostEstimate(flops=1610612736, bytes_accessed=2**21, transcendentals=6144),
    )(occ_orbitals, vir_orbitals, occ_energy.reshape(1, -1), vir_energy.reshape(1, -1), tau_points.reshape(1, -1))


def solution(mesh):
    placed = (P(("row", "col"), None), P(("row", "col"), None), P(), P(), P())
    return jax.shard_map(
        local, mesh=mesh, in_specs=placed, out_specs=P(None, "row", "col"), check_vma=False
    )
```

```python
import jax
import jax.numpy as jnp
from jax import lax
from jax.experimental import pallas as pl
from jax.experimental.pallas import tpu as pltpu
from jax.sharding import PartitionSpec as P

SLICES = 8
OCC_W = 256
VIR_W = 128
WIDTH = OCC_W + VIR_W
BLOCK = 16
ROWS = 256
COLS = 512
RUN = 4
NTAU = 2
MESH = pl.DeviceIdType.MESH


def gather_and_multiply(
    occ_hbm, vir_hbm, occ_energy_hbm, vir_energy_hbm, tau_hbm, out_ref,
    occ, vir, occ_energy, vir_energy, tau, own, scattered, lined, rows, cols, scales, total_occ, total_vir,
    in_sem, y_send, y_recv, x_send, x_recv, z_send, z_recv, up_send, up_recv, down_send, down_recv,
    pair_send, pair_recv, row_send, row_recv, core_send, core_recv, own_sem, go,
):
    row, col = lax.axis_index("row"), lax.axis_index("col")
    y, z_lo = row // RUN, row % RUN
    x, z_hi, core = col // 4, col // 2 % 2, col % 2

    def at_y(steps):
        return ((row + RUN * steps) % (SLICES * RUN), col)

    def at_x(steps):
        return (row, (col + 4 * steps) % 16)

    over = col + 2 - 4 * z_hi
    across = (row, over)
    sibling = (row, col + 1 - 2 * core)
    pair = (y * RUN + z_lo + 1 - 2 * (z_lo % 2), col)

    parity, owner = z_lo % 2, z_lo // 2

    def spread(half, to):
        return (y * RUN + to, 4 * x + 2 * half + owner)

    def early_source(source_core):
        return (y * RUN + 2 * core + parity, 4 * x + source_core)

    def late_source(p, source_core):
        return (y * RUN + 2 * core + p, 4 * x + 2 + source_core)

    early, late = z_hi == 0, z_hi == 1

    inputs = [
        pltpu.make_async_copy(src, dst, in_sem.at[i])
        for i, (src, dst) in enumerate((
            (occ_hbm, occ), (vir_hbm, vir), (occ_energy_hbm, occ_energy), (vir_energy_hbm, vir_energy), (tau_hbm, tau),
        ))
    ]
    for copy in inputs:
        copy.start()

    barrier = pltpu.get_barrier_semaphore()
    lates = [late_source(p, c) for p in range(2) for c in range(2)]
    earlies = [early_source(c) for c in range(2)]
    partners = [at_y(s) for s in (4, 3, 5, 2, 6, 1, 7)] + [at_x(s) for s in (2, 1, 3)] + [pair, sibling]

    def signal(semaphore, places):
        for place in places:
            pl.semaphore_signal(semaphore, inc=1, device_id=place, device_id_type=MESH)

    signal(barrier, partners)

    @pl.when(early)
    def _():
        signal(barrier, [across] + lates + earlies + [spread(1, parity + 2 * i) for i in range(2)])

    @pl.when(late)
    def _():
        signal(barrier, lates)

    inputs[0].wait()
    inputs[1].wait()
    for j in range(SLICES):
        own[j, :, :OCC_W] = occ[:, j * OCC_W:(j + 1) * OCC_W]
        own[j, :, OCC_W:] = vir[:, j * VIR_W:(j + 1) * VIR_W]
    pl.semaphore_wait(barrier, len(partners) + 2 + 9 * z_hi)

    @pl.when(late)
    def _():
        signal(go, [across] + earlies)


    def remote(src, dst, send, recv, place):
        return pltpu.make_async_remote_copy(
            src_ref=src, dst_ref=dst, send_sem=send, recv_sem=recv, device_id=place, device_id_type=MESH
        )

    sent = []

    def launch(build, *args):
        sent.append((build, args))
        build(*args).start()

    def send(*args):
        launch(remote, *args)

    def arrived(ref, sem):
        pltpu.make_async_copy(ref, ref, sem).wait()

    for steps in (1, 7, 2, 6, 3, 5, 4):
        send(own.at[(y + steps) % SLICES], scattered.at[y], y_send.at[steps], y_recv, at_y(steps))
    pltpu.make_async_copy(own.at[y], scattered.at[y], y_recv).start()

    def row_spot(c):
        return rows.at[:, pl.ds(pl.multiple_of(c * BLOCK, BLOCK), BLOCK)]

    row_across = remote(own, row_spot(col), row_send.at[0, 0], row_recv.at[0, 0], across)
    sent.append((lambda: row_across, ()))

    @pl.when(late)
    def _():
        row_across.start()

    send(own, row_spot(col), core_send.at[0], core_recv.at[0], sibling)
    own_copy = pltpu.make_async_copy(own, row_spot(col), own_sem)
    own_copy.start()

    for i in range(2, 5):
        inputs[i].wait()
    for j in range(SLICES):
        for t in range(NTAU):
            tau_at = tau[:, t:t + 1]
            scales[j, t:t + 1, :OCC_W] = jnp.exp(tau_at * occ_energy[:, j * OCC_W:(j + 1) * OCC_W])
            scales[j, t:t + 1, OCC_W:] = jnp.exp(-tau_at * vir_energy[:, j * VIR_W:(j + 1) * VIR_W])

    arrived(scattered, y_recv)
    for steps in (1, 3, 2):
        there = (x + steps) % 4
        send(scattered.at[pl.ds(2 * there, 2)], lined.at[:, x], x_send.at[steps], x_recv, at_x(steps))
    pltpu.make_async_copy(scattered.at[pl.ds(2 * x, 2)], lined.at[:, x], x_recv).start()

    arrived(lined, x_recv)
    spread_copies = []

    def spread_out(kind, half, to, active, slot):
        place = spread(half, to)
        spot = cols.at[y, parity, :, z_hi, pl.ds(pl.multiple_of(core * BLOCK, BLOCK), BLOCK)]
        here = jnp.logical_and(place[0] == row, place[1] == col)
        copy = remote(lined.at[half], spot, z_send.at[slot], z_recv.at[kind], place)
        there = jnp.logical_and(active, jnp.logical_not(here))
        spread_copies.append((there, copy))

        @pl.when(jnp.logical_and(active, here))
        def _():
            pltpu.make_async_copy(lined.at[half], spot, z_recv.at[kind]).start()

        @pl.when(there)
        def _():
            copy.start()

    for i in range(2):
        spread_out(0, 0, parity + 2 * i, early, i)
    for to in range(RUN):
        for half in range(2):
            spread_out(1 + parity, half, to, late, 4 + 2 * to + half)

    def to_late_half():
        @pl.when(early)
        def _():
            pl.semaphore_wait(go, 3)

        for i in range(2):
            spread_out(0, 1, parity + 2 * i, early, 2 + i)

    def early_row_across():
        @pl.when(early)
        def _():
            row_across.start()

    def chunk(j, kind, xs=slice(0, 4)):
        p = (parity, 0, 1, 1 - parity)[kind]
        return cols.at[j, p, pl.ds(xs.start, xs.stop - xs.start), (0, 1, 1, 0)[kind]]

    whole, first, second = slice(0, 4), slice(0, 2), slice(2, 4)
    last_up = {0: first, 1: whole}
    last_down = {0: second, 2: whole}

    def up_copy(step, k, xs):
        ref = chunk((y + SLICES - step) % SLICES, k, xs)
        return remote(ref, ref, up_send.at[step, k], up_recv.at[step, k], at_y(1))

    def down_copy(step, k, xs):
        ref = chunk((y + step) % SLICES, k, xs)
        return remote(ref, ref, down_send.at[step, k], down_recv.at[step, k], at_y(7))

    def pair_copy(slot, xs):
        ref = chunk((y + (4 if slot == 8 else slot)) % SLICES, 0, xs)
        return remote(ref, ref, pair_send.at[slot], pair_recv.at[slot], pair)

    def pass_up(step, k, xs=whole):
        launch(up_copy, step, k, xs)

    def pass_down(step, k, xs=whole):
        launch(down_copy, step, k, xs)

    def share(slot, xs=whole):
        launch(pair_copy, slot, xs)

    def from_spread(k):
        arrived(chunk(y, k), z_recv.at[k])
        pass_up(0, k)
        pass_down(0, k)
        if k == 0:
            share(0)

    def from_below(step, k):
        xs = whole if step < 3 else last_up[k]
        j = (y + SLICES - step - 1) % SLICES
        arrived(chunk(j, k, xs), up_recv.at[step, k])
        if step < 2:
            pass_up(step + 1, k)
        elif step == 2 and k in last_up:
            pass_up(3, k, last_up[k])
        if k == 0:
            share(SLICES - step - 1, xs)

    def from_above(step, k):
        xs = whole if step < 3 else last_down[k]
        j = (y + step + 1) % SLICES
        arrived(chunk(j, k, xs), down_recv.at[step, k])
        if step < 2:
            pass_down(step + 1, k)
        elif step == 2 and k in last_down:
            pass_down(3, k, last_down[k])
        if k == 0:
            share(step + 1 if step < 3 else 8, xs)

    def from_both(step, k):
        from_below(step, k)
        from_above(step, k)

    def only(half, step, k):
        count = len(sent)

        @pl.when(half)
        def _():
            from_both(step, k)
        again = sent[count:]
        del sent[count:]
        return again

    contract = (((1,), (1,)), ((), ()))

    def grams(j, t):
        panel = rows[j].astype(jnp.float32)
        weighted = (panel * scales[j, pl.ds(t, 1), :]).astype(jnp.bfloat16)
        columns = cols[j].reshape(COLS, WIDTH)
        gram_occ = lax.dot_general(
            weighted[:, :OCC_W], columns[:, :OCC_W], contract, preferred_element_type=jnp.float32
        )
        gram_vir = lax.dot_general(
            weighted[:, OCC_W:], columns[:, OCC_W:], contract, preferred_element_type=jnp.float32
        )
        return gram_occ, gram_vir

    def accumulate(distance):
        j = (y + distance) % SLICES
        arrived(chunk(j, 3), pair_recv.at[distance])

        @pl.loop(0, NTAU)
        def _(t):
            gram_occ, gram_vir = grams(j, t)
            if distance == 0:
                total_occ[t] = gram_occ
                total_vir[t] = gram_vir
            else:
                total_occ[t] += gram_occ
                total_vir[t] += gram_vir

    def rows_from_across():
        arrived(row_spot(over), row_recv.at[0, 0])
        for steps in (1, 3, 2):
            send(row_spot(over), row_spot(over), row_send.at[1, steps], row_recv.at[1, steps], at_x(steps))
        send(row_spot(over), row_spot(over), core_send.at[1], core_recv.at[1], sibling)

    def rows_from_beside(which):
        for i, steps in enumerate((1, 3, 2)):
            c = ((over if which else col) + 16 - 4 * steps) % 16
            arrived(row_spot(c), row_recv.at[which, steps])
            slot = 2 + 3 * which + i
            send(row_spot(c), row_spot(c), core_send.at[slot], core_recv.at[slot], sibling)

    def rows_complete():
        own_copy.wait()
        for slot in range(8):
            arrived(row_spot(col), core_recv.at[slot])

    to_late_half()
    from_spread(0)
    from_both(0, 0)
    early_row_across()
    sent += only(early, 1, 0)
    from_spread(1)
    for steps in (1, 3, 2):
        send(own, row_spot(col), row_send.at[0, steps], row_recv.at[0, steps], at_x(steps))
    from_spread(2)
    rows_from_across()
    sent += only(early, 2, 0)
    only(late, 1, 0)
    rows_from_beside(0)
    from_both(0, 1)
    from_both(0, 2)
    only(late, 2, 0)
    rows_from_beside(1)
    from_both(1, 1)
    from_both(1, 2)
    rows_complete()
    for distance in (0, 1, 7):
        accumulate(distance)
    from_both(3, 0)
    from_both(2, 1)
    from_both(2, 2)
    for distance in (2, 6, 3, 5):
        accumulate(distance)
    from_below(3, 1)
    from_above(3, 2)

    last = (y + 4) % SLICES
    arrived(chunk(last, 3, first), pair_recv.at[4])
    arrived(chunk(last, 3, second), pair_recv.at[8])
    for t in range(NTAU):
        gram_occ, gram_vir = grams(last, t)
        out_ref[t] = -((total_occ[t] + gram_occ) * (total_vir[t] + gram_vir))

    for build, args in sent:
        build(*args).wait_send()
    for there, copy in spread_copies:
        @pl.when(there)
        def _():
            copy.wait_send()


def local(occ_orbitals, vir_orbitals, occ_energy, vir_energy, tau_points):
    dma = pltpu.SemaphoreType.DMA
    place = pl.BlockSpec(memory_space=pl.ANY)
    bf16, f32 = jnp.bfloat16, jnp.float32
    operands = (occ_orbitals, vir_orbitals, occ_energy.reshape(1, -1), vir_energy.reshape(1, -1), tau_points.reshape(1, -1))
    return pl.pallas_call(
        gather_and_multiply,
        out_shape=jax.ShapeDtypeStruct((NTAU, ROWS, COLS), f32),
        in_specs=[place] * 5,
        out_specs=pl.BlockSpec(memory_space=pltpu.VMEM),
        scratch_shapes=[
            pltpu.VMEM(occ_orbitals.shape, bf16),
            pltpu.VMEM(vir_orbitals.shape, bf16),
            pltpu.VMEM((1, SLICES * OCC_W), f32),
            pltpu.VMEM((1, SLICES * VIR_W), f32),
            pltpu.VMEM((1, NTAU), f32),
            pltpu.VMEM((SLICES, BLOCK, WIDTH), bf16),
            pltpu.VMEM((SLICES, BLOCK, WIDTH), bf16),
            pltpu.VMEM((2, 4, BLOCK, WIDTH), bf16),
            pltpu.VMEM((SLICES, ROWS, WIDTH), bf16),
            pltpu.VMEM((SLICES, 2, 4, 2, 2 * BLOCK, WIDTH), bf16),
            pltpu.VMEM((SLICES, NTAU, WIDTH), f32),
            pltpu.VMEM((NTAU, ROWS, COLS), f32),
            pltpu.VMEM((NTAU, ROWS, COLS), f32),
            dma((5,)),
            dma((SLICES,)), dma,
            dma((4,)), dma,
            dma((12,)), dma((3,)),
            dma((4, 3)), dma((4, 3)),
            dma((4, 3)), dma((4, 3)),
            dma((SLICES + 1,)), dma((SLICES + 1,)),
            dma((2, 4)), dma((2, 4)),
            dma((8,)), dma((8,)),
            dma,
            pltpu.SemaphoreType.REGULAR,
        ],
        compiler_params=pltpu.CompilerParams(
            collective_id=0, has_side_effects=True, vmem_limit_bytes=40 * 2**20
        ),
        cost_estimate=pl.CostEstimate(flops=1610612736, bytes_accessed=2**21, transcendentals=6144),
    )(*[pltpu.with_memory_space_constraint(operand, pltpu.HBM) for operand in operands])


def solution(mesh):
    placed = (P(("row", "col"), None), P(("row", "col"), None), P(), P(), P())
    return jax.shard_map(
        local, mesh=mesh, in_specs=placed, out_specs=P(None, "row", "col"), check_vma=False
    )
```

```python
import jax
import jax.numpy as jnp
from jax import lax
from jax.experimental import pallas as pl
from jax.experimental.pallas import tpu as pltpu
from jax.sharding import PartitionSpec as P

SLICES = 8
OCC_W = 256
VIR_W = 128
WIDTH = OCC_W + VIR_W
BLOCK = 16
ROWS = 256
COLS = 512
RUN = 4
NTAU = 2
MESH = pl.DeviceIdType.MESH


def gather_and_multiply(
    occ_hbm, vir_hbm, occ_energy_hbm, vir_energy_hbm, tau_hbm, out_ref,
    occ, vir, occ_energy, vir_energy, tau, own, scattered, lined, rows, cols, scales, total_occ, total_vir,
    in_sem, y_send, y_recv, x_send, x_recv, z_send, z_recv, up_send, up_recv, down_send, down_recv,
    pair_send, pair_recv, row_send, row_recv, core_send, core_recv, own_sem, go, straight_send,
):
    row, col = lax.axis_index("row"), lax.axis_index("col")
    y, z_lo = row // RUN, row % RUN
    x, z_hi, core = col // 4, col // 2 % 2, col % 2

    def at_y(steps):
        return ((row + RUN * steps) % (SLICES * RUN), col)

    def at_x(steps):
        return (row, (col + 4 * steps) % 16)

    over = col + 2 - 4 * z_hi
    across = (row, over)
    sibling = (row, col + 1 - 2 * core)
    pair = (y * RUN + z_lo + 1 - 2 * (z_lo % 2), col)

    parity, owner = z_lo % 2, z_lo // 2

    def spread(half, to):
        return (y * RUN + to, 4 * x + 2 * half + owner)

    def early_source(source_core):
        return (y * RUN + 2 * core + parity, 4 * x + source_core)

    def late_source(p, source_core):
        return (y * RUN + 2 * core + p, 4 * x + 2 + source_core)

    early, late = z_hi == 0, z_hi == 1

    inputs = [
        pltpu.make_async_copy(src, dst, in_sem.at[i])
        for i, (src, dst) in enumerate((
            (occ_hbm, occ), (vir_hbm, vir), (occ_energy_hbm, occ_energy), (vir_energy_hbm, vir_energy), (tau_hbm, tau),
        ))
    ]
    for copy in inputs:
        copy.start()

    barrier = pltpu.get_barrier_semaphore()
    lates = [late_source(p, c) for p in range(2) for c in range(2)]
    earlies = [early_source(c) for c in range(2)]
    partners = [at_y(s) for s in (4, 3, 5, 2, 6, 1, 7)] + [at_x(s) for s in (2, 1, 3)] + [pair, sibling]

    def signal(semaphore, places):
        for place in places:
            pl.semaphore_signal(semaphore, inc=1, device_id=place, device_id_type=MESH)

    signal(barrier, partners)

    straight = jnp.logical_and(late, y % 2 == 0)
    scatters = jnp.logical_or(early, y % 2 == 1)

    def straight_place(j, to):
        return (j * RUN + to, 4 * (y // 2) + owner)

    @pl.when(early)
    def _():
        signal(barrier, [across] + earlies + [spread(1, parity + 2 * i) for i in range(2)])
        signal(barrier, [(2 * x * RUN + 2 * core + p, 4 * there + 2 + c) for p in range(2) for there in range(4) for c in range(2)])

    @pl.when(late)
    def _():
        signal(barrier, lates)

    inputs[0].wait()
    inputs[1].wait()
    for j in range(SLICES):
        own[j, :, :OCC_W] = occ[:, j * OCC_W:(j + 1) * OCC_W]
        own[j, :, OCC_W:] = vir[:, j * VIR_W:(j + 1) * VIR_W]
    pl.semaphore_wait(barrier, len(partners) + 2 + 5 * z_hi + 32 * z_hi * (1 - y % 2))

    @pl.when(late)
    def _():
        signal(go, [across] + earlies)


    def remote(src, dst, send, recv, place):
        return pltpu.make_async_remote_copy(
            src_ref=src, dst_ref=dst, send_sem=send, recv_sem=recv, device_id=place, device_id_type=MESH
        )

    sent = []

    def launch(build, *args):
        sent.append((build, args))
        build(*args).start()

    def send(*args):
        launch(remote, *args)

    def arrived(ref, sem):
        pltpu.make_async_copy(ref, ref, sem).wait()

    def scatter_copy(steps):
        return remote(own.at[(y + steps) % SLICES], scattered.at[y], y_send.at[steps], y_recv, at_y(steps))

    around = (1, 7, 2, 6, 3, 5, 4)

    @pl.when(scatters)
    def _():
        for steps in around:
            scatter_copy(steps).start()
        pltpu.make_async_copy(own.at[y], scattered.at[y], y_recv).start()

    def straight_copy(j, to):
        spot = cols.at[j, parity, x, 1, pl.ds(pl.multiple_of(core * BLOCK, BLOCK), BLOCK)]
        return remote(own.at[j], spot, straight_send.at[j, to], z_recv.at[1 + parity], straight_place(j, to))

    @pl.when(straight)
    def _():
        for to in (0, 3, 1, 2):
            for j in range(SLICES):
                straight_copy(j, to).start()

    def row_spot(c):
        return rows.at[:, pl.ds(pl.multiple_of(c * BLOCK, BLOCK), BLOCK)]

    row_across = remote(own, row_spot(col), row_send.at[0, 0], row_recv.at[0, 0], across)
    sent.append((lambda: row_across, ()))

    @pl.when(late)
    def _():
        row_across.start()

    send(own, row_spot(col), core_send.at[0], core_recv.at[0], sibling)
    own_copy = pltpu.make_async_copy(own, row_spot(col), own_sem)
    own_copy.start()

    for i in range(2, 5):
        inputs[i].wait()
    for j in range(SLICES):
        for t in range(NTAU):
            tau_at = tau[:, t:t + 1]
            scales[j, t:t + 1, :OCC_W] = jnp.exp(tau_at * occ_energy[:, j * OCC_W:(j + 1) * OCC_W])
            scales[j, t:t + 1, OCC_W:] = jnp.exp(-tau_at * vir_energy[:, j * VIR_W:(j + 1) * VIR_W])

    def pair_of_planes(steps):
        there = (x + steps) % 4
        return scattered.at[pl.ds(2 * there, 2)], lined.at[:, x]

    def odd_plane(steps):
        there = (x + steps) % 4
        return scattered.at[2 * there + 1], lined.at[1, x]

    def exchange_copy(parts, steps):
        src, dst = parts(steps)
        return remote(src, dst, x_send.at[steps], x_recv, at_x(steps))

    def exchange(parts):
        for steps in (1, 3, 2):
            exchange_copy(parts, steps).start()
        src, dst = parts(0)
        pltpu.make_async_copy(src, dst, x_recv).start()

    @pl.when(early)
    def _():
        arrived(scattered, y_recv)
        exchange(pair_of_planes)
        arrived(lined, x_recv)

    @pl.when(late)
    def _():
        arrived(scattered.at[pl.ds(0, 4)], y_recv)
        exchange(odd_plane)
        arrived(lined.at[0], x_recv)

    spread_copies = []

    def spread_out(kind, half, to, active, slot):
        place = spread(half, to)
        spot = cols.at[y, parity, :, z_hi, pl.ds(pl.multiple_of(core * BLOCK, BLOCK), BLOCK)]
        here = jnp.logical_and(place[0] == row, place[1] == col)
        copy = remote(lined.at[half], spot, z_send.at[slot], z_recv.at[kind], place)
        there = jnp.logical_and(active, jnp.logical_not(here))
        spread_copies.append((there, copy))

        @pl.when(jnp.logical_and(active, here))
        def _():
            pltpu.make_async_copy(lined.at[half], spot, z_recv.at[kind]).start()

        @pl.when(there)
        def _():
            copy.start()

    for i in range(2):
        spread_out(0, 0, parity + 2 * i, early, i)
    for to in range(RUN):
        spread_out(1 + parity, 1, to, late, 4 + 2 * to + 1)

    def to_late_half():
        @pl.when(early)
        def _():
            pl.semaphore_wait(go, 3)

        for i in range(2):
            spread_out(0, 1, parity + 2 * i, early, 2 + i)

    def early_row_across():
        @pl.when(early)
        def _():
            row_across.start()

    def chunk(j, kind, xs=slice(0, 4)):
        p = (parity, 0, 1, 1 - parity)[kind]
        return cols.at[j, p, pl.ds(xs.start, xs.stop - xs.start), (0, 1, 1, 0)[kind]]

    whole, first, second = slice(0, 4), slice(0, 2), slice(2, 4)
    last_up = {0: first, 1: whole}
    last_down = {0: second, 2: whole}

    def up_copy(step, k, xs):
        ref = chunk((y + SLICES - step) % SLICES, k, xs)
        return remote(ref, ref, up_send.at[step, k], up_recv.at[step, k], at_y(1))

    def down_copy(step, k, xs):
        ref = chunk((y + step) % SLICES, k, xs)
        return remote(ref, ref, down_send.at[step, k], down_recv.at[step, k], at_y(7))

    def pair_copy(slot, xs):
        ref = chunk((y + (4 if slot == 8 else slot)) % SLICES, 0, xs)
        return remote(ref, ref, pair_send.at[slot], pair_recv.at[slot], pair)

    def pass_up(step, k, xs=whole):
        launch(up_copy, step, k, xs)

    def pass_down(step, k, xs=whole):
        launch(down_copy, step, k, xs)

    at_once = (z_lo % 3 == 0) == late

    def share(slot, xs=whole):
        @pl.when(at_once)
        def _():
            pair_copy(slot, xs).start()

    def share_later(slot, xs=whole):
        sent.append((pair_copy, (slot, xs)))

        @pl.when(jnp.logical_not(at_once))
        def _():
            pair_copy(slot, xs).start()

    def from_spread(k):
        arrived(chunk(y, k), z_recv.at[k])
        pass_up(0, k)
        pass_down(0, k)
        if k == 0:
            share(0)

    def from_below(step, k):
        xs = whole if step < 3 else last_up[k]
        j = (y + SLICES - step - 1) % SLICES
        arrived(chunk(j, k, xs), up_recv.at[step, k])
        if step < 2:
            pass_up(step + 1, k)
        elif step == 2 and k in last_up:
            pass_up(3, k, last_up[k])
        if k == 0:
            share(SLICES - step - 1, xs)

    def from_above(step, k):
        xs = whole if step < 3 else last_down[k]
        j = (y + step + 1) % SLICES
        arrived(chunk(j, k, xs), down_recv.at[step, k])
        if step < 2:
            pass_down(step + 1, k)
        elif step == 2 and k in last_down:
            pass_down(3, k, last_down[k])
        if k == 0:
            share(step + 1 if step < 3 else 8, xs)

    def from_both(step, k):
        from_below(step, k)
        from_above(step, k)

    def only(half, step, k):
        count = len(sent)

        @pl.when(half)
        def _():
            from_both(step, k)
        again = sent[count:]
        del sent[count:]
        return again

    contract = (((1,), (1,)), ((), ()))

    def grams(j, t):
        panel = rows[j].astype(jnp.float32)
        weighted = (panel * scales[j, pl.ds(t, 1), :]).astype(jnp.bfloat16)
        columns = cols[j].reshape(COLS, WIDTH)
        gram_occ = lax.dot_general(
            weighted[:, :OCC_W], columns[:, :OCC_W], contract, preferred_element_type=jnp.float32
        )
        gram_vir = lax.dot_general(
            weighted[:, OCC_W:], columns[:, OCC_W:], contract, preferred_element_type=jnp.float32
        )
        return gram_occ, gram_vir

    def accumulate(distance):
        j = (y + distance) % SLICES
        arrived(chunk(j, 3), pair_recv.at[distance])

        @pl.loop(0, NTAU)
        def _(t):
            gram_occ, gram_vir = grams(j, t)
            if distance == 0:
                total_occ[t] = gram_occ
                total_vir[t] = gram_vir
            else:
                total_occ[t] += gram_occ
                total_vir[t] += gram_vir

    def rows_from_across():
        arrived(row_spot(over), row_recv.at[0, 0])
        for steps in (1, 3, 2):
            send(row_spot(over), row_spot(over), row_send.at[1, steps], row_recv.at[1, steps], at_x(steps))
        send(row_spot(over), row_spot(over), core_send.at[1], core_recv.at[1], sibling)

    def rows_from_beside(which):
        for i, steps in enumerate((1, 3, 2)):
            c = ((over if which else col) + 16 - 4 * steps) % 16
            arrived(row_spot(c), row_recv.at[which, steps])
            slot = 2 + 3 * which + i
            send(row_spot(c), row_spot(c), core_send.at[slot], core_recv.at[slot], sibling)

    def rows_complete():
        own_copy.wait()
        for slot in range(8):
            arrived(row_spot(col), core_recv.at[slot])

    to_late_half()
    from_spread(0)
    from_both(0, 0)
    early_row_across()
    sent += only(early, 1, 0)
    from_spread(1)
    for steps in (1, 3, 2):
        send(own, row_spot(col), row_send.at[0, steps], row_recv.at[0, steps], at_x(steps))
    from_spread(2)
    for slot in (0, 1, 7):
        share_later(slot)
    rows_from_across()
    sent += only(early, 2, 0)
    only(late, 1, 0)
    share_later(2)
    share_later(6)
    rows_from_beside(0)
    from_both(0, 1)
    from_both(0, 2)
    only(late, 2, 0)
    share_later(3)
    share_later(5)
    rows_from_beside(1)
    from_both(1, 1)
    from_both(1, 2)
    rows_complete()
    for distance in (0, 1, 7):
        accumulate(distance)
    from_both(3, 0)
    share_later(4, first)
    share_later(8, second)
    from_both(2, 1)
    from_both(2, 2)
    for distance in (2, 6, 3, 5):
        accumulate(distance)
    from_below(3, 1)
    from_above(3, 2)

    last = (y + 4) % SLICES
    arrived(chunk(last, 3, first), pair_recv.at[4])
    arrived(chunk(last, 3, second), pair_recv.at[8])
    for t in range(NTAU):
        gram_occ, gram_vir = grams(last, t)
        out_ref[t] = -((total_occ[t] + gram_occ) * (total_vir[t] + gram_vir))

    for build, args in sent:
        build(*args).wait_send()
    @pl.when(scatters)
    def _():
        for steps in around:
            scatter_copy(steps).wait_send()

    @pl.when(straight)
    def _():
        for j in range(SLICES):
            for to in range(RUN):
                straight_copy(j, to).wait_send()

    for steps in (1, 3, 2):
        @pl.when(early)
        def _():
            exchange_copy(pair_of_planes, steps).wait_send()

        @pl.when(late)
        def _():
            exchange_copy(odd_plane, steps).wait_send()

    for there, copy in spread_copies:
        @pl.when(there)
        def _():
            copy.wait_send()


def local(occ_orbitals, vir_orbitals, occ_energy, vir_energy, tau_points):
    dma = pltpu.SemaphoreType.DMA
    place = pl.BlockSpec(memory_space=pl.ANY)
    bf16, f32 = jnp.bfloat16, jnp.float32
    operands = (occ_orbitals, vir_orbitals, occ_energy.reshape(1, -1), vir_energy.reshape(1, -1), tau_points.reshape(1, -1))
    return pl.pallas_call(
        gather_and_multiply,
        out_shape=jax.ShapeDtypeStruct((NTAU, ROWS, COLS), f32),
        in_specs=[place] * 5,
        out_specs=pl.BlockSpec(memory_space=pltpu.VMEM),
        scratch_shapes=[
            pltpu.VMEM(occ_orbitals.shape, bf16),
            pltpu.VMEM(vir_orbitals.shape, bf16),
            pltpu.VMEM((1, SLICES * OCC_W), f32),
            pltpu.VMEM((1, SLICES * VIR_W), f32),
            pltpu.VMEM((1, NTAU), f32),
            pltpu.VMEM((SLICES, BLOCK, WIDTH), bf16),
            pltpu.VMEM((SLICES, BLOCK, WIDTH), bf16),
            pltpu.VMEM((2, 4, BLOCK, WIDTH), bf16),
            pltpu.VMEM((SLICES, ROWS, WIDTH), bf16),
            pltpu.VMEM((SLICES, 2, 4, 2, 2 * BLOCK, WIDTH), bf16),
            pltpu.VMEM((SLICES, NTAU, WIDTH), f32),
            pltpu.VMEM((NTAU, ROWS, COLS), f32),
            pltpu.VMEM((NTAU, ROWS, COLS), f32),
            dma((5,)),
            dma((SLICES,)), dma,
            dma((4,)), dma,
            dma((12,)), dma((3,)),
            dma((4, 3)), dma((4, 3)),
            dma((4, 3)), dma((4, 3)),
            dma((SLICES + 1,)), dma((SLICES + 1,)),
            dma((2, 4)), dma((2, 4)),
            dma((8,)), dma((8,)),
            dma,
            pltpu.SemaphoreType.REGULAR,
            dma((SLICES, RUN)),
        ],
        compiler_params=pltpu.CompilerParams(
            collective_id=0, has_side_effects=True, vmem_limit_bytes=40 * 2**20
        ),
        cost_estimate=pl.CostEstimate(flops=1610612736, bytes_accessed=2**21, transcendentals=6144),
    )(*[pltpu.with_memory_space_constraint(operand, pltpu.HBM) for operand in operands])


def solution(mesh):
    placed = (P(("row", "col"), None), P(("row", "col"), None), P(), P(), P())
    return jax.shard_map(
        local, mesh=mesh, in_specs=placed, out_specs=P(None, "row", "col"), check_vma=False
    )
```

```python
import jax
import jax.numpy as jnp
from jax import lax
from jax.experimental import pallas as pl
from jax.experimental.pallas import tpu as pltpu
from jax.sharding import PartitionSpec as P

SLICES = 8
OCC_W = 256
VIR_W = 128
WIDTH = OCC_W + VIR_W
BLOCK = 16
ROWS = 256
COLS = 512
RUN = 4
NTAU = 2
MESH = pl.DeviceIdType.MESH


def gather_and_multiply(
    occ_hbm, vir_hbm, occ_energy_hbm, vir_energy_hbm, tau_hbm, out_ref,
    occ, vir, occ_energy, vir_energy, tau, own, scattered, lined, rows, cols, scales, total_occ, total_vir,
    in_sem, y_send, y_recv, x_send, x_recv, z_send, z_recv, up_send, up_recv, down_send, down_recv,
    pair_send, pair_recv, row_send, row_recv, core_send, core_recv, own_sem, go, straight_send,
):
    row, col = lax.axis_index("row"), lax.axis_index("col")
    y, z_lo = row // RUN, row % RUN
    x, z_hi, core = col // 4, col // 2 % 2, col % 2

    def at_y(steps):
        return ((row + RUN * steps) % (SLICES * RUN), col)

    def at_x(steps):
        return (row, (col + 4 * steps) % 16)

    over = col + 2 - 4 * z_hi
    across = (row, over)
    sibling = (row, col + 1 - 2 * core)
    pair = (y * RUN + z_lo + 1 - 2 * (z_lo % 2), col)

    parity, owner = z_lo % 2, z_lo // 2

    def spread(half, to):
        return (y * RUN + to, 4 * x + 2 * half + owner)

    def early_source(source_core):
        return (y * RUN + 2 * core + parity, 4 * x + source_core)

    def late_source(p, source_core):
        return (y * RUN + 2 * core + p, 4 * x + 2 + source_core)

    early, late = z_hi == 0, z_hi == 1

    inputs = [
        pltpu.make_async_copy(src, dst, in_sem.at[i])
        for i, (src, dst) in enumerate((
            (occ_hbm, occ), (vir_hbm, vir), (occ_energy_hbm, occ_energy), (vir_energy_hbm, vir_energy), (tau_hbm, tau),
        ))
    ]
    for copy in inputs:
        copy.start()

    barrier = pltpu.get_barrier_semaphore()
    lates = [late_source(p, c) for p in range(2) for c in range(2)]
    earlies = [early_source(c) for c in range(2)]
    partners = [at_y(s) for s in (4, 3, 5, 2, 6, 1, 7)] + [at_x(s) for s in (2, 1, 3)] + [pair, sibling]

    def signal(semaphore, places):
        for place in places:
            pl.semaphore_signal(semaphore, inc=1, device_id=place, device_id_type=MESH)

    signal(barrier, partners)

    straight = jnp.logical_and(late, y % 2 == 0)
    scatters = jnp.logical_or(early, y % 2 == 1)

    def straight_place(j, to):
        return (j * RUN + to, 4 * (y // 2) + owner)

    @pl.when(early)
    def _():
        signal(barrier, [across] + earlies + [spread(1, parity + 2 * i) for i in range(2)])
        signal(barrier, [(2 * x * RUN + 2 * core + p, 4 * there + 2 + c) for p in range(2) for there in range(4) for c in range(2)])

    @pl.when(late)
    def _():
        signal(barrier, lates)

    inputs[0].wait()
    inputs[1].wait()
    for j in range(SLICES):
        own[j, :, :OCC_W] = occ[:, j * OCC_W:(j + 1) * OCC_W]
        own[j, :, OCC_W:] = vir[:, j * VIR_W:(j + 1) * VIR_W]
    pl.semaphore_wait(barrier, len(partners) + 2 + 5 * z_hi + 32 * z_hi * (1 - y % 2))

    @pl.when(late)
    def _():
        signal(go, [across] + earlies)


    def remote(src, dst, send, recv, place):
        return pltpu.make_async_remote_copy(
            src_ref=src, dst_ref=dst, send_sem=send, recv_sem=recv, device_id=place, device_id_type=MESH
        )

    sent = []

    def launch(build, *args):
        sent.append((build, args))
        build(*args).start()

    def send(*args):
        launch(remote, *args)

    def arrived(ref, sem):
        pltpu.make_async_copy(ref, ref, sem).wait()

    def scatter_copy(steps):
        return remote(own.at[(y + steps) % SLICES], scattered.at[y], y_send.at[steps], y_recv, at_y(steps))

    around = (4, 3, 5, 2, 6, 1, 7)

    @pl.when(scatters)
    def _():
        for steps in around:
            scatter_copy(steps).start()
        pltpu.make_async_copy(own.at[y], scattered.at[y], y_recv).start()

    def straight_copy(j, to):
        spot = cols.at[j, parity, x, 1, pl.ds(pl.multiple_of(core * BLOCK, BLOCK), BLOCK)]
        return remote(own.at[j], spot, straight_send.at[j, to], z_recv.at[1 + parity], straight_place(j, to))

    @pl.when(straight)
    def _():
        for to in (0, 3, 1, 2):
            for j in range(SLICES):
                straight_copy(j, to).start()

    def row_spot(c):
        return rows.at[:, pl.ds(pl.multiple_of(c * BLOCK, BLOCK), BLOCK)]

    row_across = remote(own, row_spot(col), row_send.at[0, 0], row_recv.at[0, 0], across)
    sent.append((lambda: row_across, ()))

    @pl.when(late)
    def _():
        row_across.start()

    send(own, row_spot(col), core_send.at[0], core_recv.at[0], sibling)
    own_copy = pltpu.make_async_copy(own, row_spot(col), own_sem)
    own_copy.start()

    for i in range(2, 5):
        inputs[i].wait()
    for j in range(SLICES):
        for t in range(NTAU):
            tau_at = tau[:, t:t + 1]
            scales[j, t:t + 1, :OCC_W] = jnp.exp(tau_at * occ_energy[:, j * OCC_W:(j + 1) * OCC_W])
            scales[j, t:t + 1, OCC_W:] = jnp.exp(-tau_at * vir_energy[:, j * VIR_W:(j + 1) * VIR_W])

    def pair_of_planes(steps):
        there = (x + steps) % 4
        return scattered.at[pl.ds(2 * there, 2)], lined.at[:, x]

    def odd_plane(steps):
        there = (x + steps) % 4
        return scattered.at[2 * there + 1], lined.at[1, x]

    def exchange_copy(parts, steps):
        src, dst = parts(steps)
        return remote(src, dst, x_send.at[steps], x_recv, at_x(steps))

    def exchange(parts):
        for steps in (1, 3, 2):
            exchange_copy(parts, steps).start()
        src, dst = parts(0)
        pltpu.make_async_copy(src, dst, x_recv).start()

    @pl.when(early)
    def _():
        arrived(scattered, y_recv)
        exchange(pair_of_planes)
        arrived(lined, x_recv)

    @pl.when(late)
    def _():
        arrived(scattered.at[pl.ds(0, 4)], y_recv)
        exchange(odd_plane)
        arrived(lined.at[0], x_recv)

    spread_copies = []

    def spread_out(kind, half, to, active, slot):
        place = spread(half, to)
        spot = cols.at[y, parity, :, z_hi, pl.ds(pl.multiple_of(core * BLOCK, BLOCK), BLOCK)]
        here = jnp.logical_and(place[0] == row, place[1] == col)
        copy = remote(lined.at[half], spot, z_send.at[slot], z_recv.at[kind], place)
        there = jnp.logical_and(active, jnp.logical_not(here))
        spread_copies.append((there, copy))

        @pl.when(jnp.logical_and(active, here))
        def _():
            pltpu.make_async_copy(lined.at[half], spot, z_recv.at[kind]).start()

        @pl.when(there)
        def _():
            copy.start()

    for i in range(2):
        spread_out(0, 0, parity + 2 * i, early, i)
    for to in range(RUN):
        spread_out(1 + parity, 1, to, late, 4 + 2 * to + 1)

    def to_late_half():
        @pl.when(early)
        def _():
            pl.semaphore_wait(go, 3)

        for i in range(2):
            spread_out(0, 1, parity + 2 * i, early, 2 + i)

    def early_row_across():
        @pl.when(early)
        def _():
            row_across.start()

    def chunk(j, kind, xs=slice(0, 4)):
        p = (parity, 0, 1, 1 - parity)[kind]
        return cols.at[j, p, pl.ds(xs.start, xs.stop - xs.start), (0, 1, 1, 0)[kind]]

    whole, first, second = slice(0, 4), slice(0, 2), slice(2, 4)
    last_up = {0: first, 1: whole}
    last_down = {0: second, 2: whole}

    def up_copy(step, k, xs):
        ref = chunk((y + SLICES - step) % SLICES, k, xs)
        return remote(ref, ref, up_send.at[step, k], up_recv.at[step, k], at_y(1))

    def down_copy(step, k, xs):
        ref = chunk((y + step) % SLICES, k, xs)
        return remote(ref, ref, down_send.at[step, k], down_recv.at[step, k], at_y(7))

    def pair_copy(slot, xs):
        ref = chunk((y + (4 if slot == 8 else slot)) % SLICES, 0, xs)
        return remote(ref, ref, pair_send.at[slot], pair_recv.at[slot], pair)

    def pass_up(step, k, xs=whole):
        launch(up_copy, step, k, xs)

    def pass_down(step, k, xs=whole):
        launch(down_copy, step, k, xs)

    at_once = jnp.logical_or(late, z_lo % 3 != 0)

    def share(slot, xs=whole):
        @pl.when(at_once)
        def _():
            pair_copy(slot, xs).start()

    def share_later(slot, xs=whole):
        sent.append((pair_copy, (slot, xs)))

        @pl.when(jnp.logical_not(at_once))
        def _():
            pair_copy(slot, xs).start()

    def from_spread(k):
        arrived(chunk(y, k), z_recv.at[k])
        pass_up(0, k)
        pass_down(0, k)
        if k == 0:
            share(0)

    def from_below(step, k):
        xs = whole if step < 3 else last_up[k]
        j = (y + SLICES - step - 1) % SLICES
        arrived(chunk(j, k, xs), up_recv.at[step, k])
        if step < 2:
            pass_up(step + 1, k)
        elif step == 2 and k in last_up:
            pass_up(3, k, last_up[k])
        if k == 0:
            share(SLICES - step - 1, xs)

    def from_above(step, k):
        xs = whole if step < 3 else last_down[k]
        j = (y + step + 1) % SLICES
        arrived(chunk(j, k, xs), down_recv.at[step, k])
        if step < 2:
            pass_down(step + 1, k)
        elif step == 2 and k in last_down:
            pass_down(3, k, last_down[k])
        if k == 0:
            share(step + 1 if step < 3 else 8, xs)

    def from_both(step, k):
        from_below(step, k)
        from_above(step, k)

    def only(half, step, k):
        count = len(sent)

        @pl.when(half)
        def _():
            from_both(step, k)
        again = sent[count:]
        del sent[count:]
        return again

    contract = (((1,), (1,)), ((), ()))

    def grams(j, t):
        panel = rows[j].astype(jnp.float32)
        weighted = (panel * scales[j, pl.ds(t, 1), :]).astype(jnp.bfloat16)
        columns = cols[j].reshape(COLS, WIDTH)
        gram_occ = lax.dot_general(
            weighted[:, :OCC_W], columns[:, :OCC_W], contract, preferred_element_type=jnp.float32
        )
        gram_vir = lax.dot_general(
            weighted[:, OCC_W:], columns[:, OCC_W:], contract, preferred_element_type=jnp.float32
        )
        return gram_occ, gram_vir

    def accumulate(distance):
        j = (y + distance) % SLICES
        arrived(chunk(j, 3), pair_recv.at[distance])

        @pl.loop(0, NTAU)
        def _(t):
            gram_occ, gram_vir = grams(j, t)
            if distance == 0:
                total_occ[t] = gram_occ
                total_vir[t] = gram_vir
            else:
                total_occ[t] += gram_occ
                total_vir[t] += gram_vir

    def rows_from_across():
        arrived(row_spot(over), row_recv.at[0, 0])
        for steps in (1, 3, 2):
            send(row_spot(over), row_spot(over), row_send.at[1, steps], row_recv.at[1, steps], at_x(steps))
        send(row_spot(over), row_spot(over), core_send.at[1], core_recv.at[1], sibling)

    def rows_from_beside(which):
        for i, steps in enumerate((1, 3, 2)):
            c = ((over if which else col) + 16 - 4 * steps) % 16
            arrived(row_spot(c), row_recv.at[which, steps])
            slot = 2 + 3 * which + i
            send(row_spot(c), row_spot(c), core_send.at[slot], core_recv.at[slot], sibling)

    def rows_complete():
        own_copy.wait()
        for slot in range(8):
            arrived(row_spot(col), core_recv.at[slot])

    to_late_half()
    from_spread(0)
    from_both(0, 0)
    early_row_across()
    sent += only(early, 1, 0)
    from_spread(1)
    for steps in (1, 3, 2):
        send(own, row_spot(col), row_send.at[0, steps], row_recv.at[0, steps], at_x(steps))
    from_spread(2)
    for slot in (0, 1, 7):
        share_later(slot)
    rows_from_across()
    sent += only(early, 2, 0)
    only(late, 1, 0)
    share_later(2)
    share_later(6)
    rows_from_beside(0)
    from_both(0, 1)
    from_both(0, 2)
    only(late, 2, 0)
    share_later(3)
    share_later(5)
    rows_from_beside(1)
    from_both(1, 1)
    from_both(1, 2)
    rows_complete()
    for distance in (0, 1, 7):
        accumulate(distance)
    from_both(3, 0)
    share_later(4, first)
    share_later(8, second)
    from_both(2, 1)
    from_both(2, 2)
    for distance in (2, 6, 3, 5):
        accumulate(distance)
    from_below(3, 1)
    from_above(3, 2)

    last = (y + 4) % SLICES
    arrived(chunk(last, 3, first), pair_recv.at[4])
    arrived(chunk(last, 3, second), pair_recv.at[8])
    for t in range(NTAU):
        gram_occ, gram_vir = grams(last, t)
        out_ref[t] = -((total_occ[t] + gram_occ) * (total_vir[t] + gram_vir))

    for build, args in sent:
        build(*args).wait_send()
    @pl.when(scatters)
    def _():
        for steps in around:
            scatter_copy(steps).wait_send()

    @pl.when(straight)
    def _():
        for j in range(SLICES):
            for to in range(RUN):
                straight_copy(j, to).wait_send()

    for steps in (1, 3, 2):
        @pl.when(early)
        def _():
            exchange_copy(pair_of_planes, steps).wait_send()

        @pl.when(late)
        def _():
            exchange_copy(odd_plane, steps).wait_send()

    for there, copy in spread_copies:
        @pl.when(there)
        def _():
            copy.wait_send()


def local(occ_orbitals, vir_orbitals, occ_energy, vir_energy, tau_points):
    dma = pltpu.SemaphoreType.DMA
    place = pl.BlockSpec(memory_space=pl.ANY)
    bf16, f32 = jnp.bfloat16, jnp.float32
    operands = (occ_orbitals, vir_orbitals, occ_energy.reshape(1, -1), vir_energy.reshape(1, -1), tau_points.reshape(1, -1))
    return pl.pallas_call(
        gather_and_multiply,
        out_shape=jax.ShapeDtypeStruct((NTAU, ROWS, COLS), f32),
        in_specs=[place] * 5,
        out_specs=pl.BlockSpec(memory_space=pltpu.VMEM),
        scratch_shapes=[
            pltpu.VMEM(occ_orbitals.shape, bf16),
            pltpu.VMEM(vir_orbitals.shape, bf16),
            pltpu.VMEM((1, SLICES * OCC_W), f32),
            pltpu.VMEM((1, SLICES * VIR_W), f32),
            pltpu.VMEM((1, NTAU), f32),
            pltpu.VMEM((SLICES, BLOCK, WIDTH), bf16),
            pltpu.VMEM((SLICES, BLOCK, WIDTH), bf16),
            pltpu.VMEM((2, 4, BLOCK, WIDTH), bf16),
            pltpu.VMEM((SLICES, ROWS, WIDTH), bf16),
            pltpu.VMEM((SLICES, 2, 4, 2, 2 * BLOCK, WIDTH), bf16),
            pltpu.VMEM((SLICES, NTAU, WIDTH), f32),
            pltpu.VMEM((NTAU, ROWS, COLS), f32),
            pltpu.VMEM((NTAU, ROWS, COLS), f32),
            dma((5,)),
            dma((SLICES,)), dma,
            dma((4,)), dma,
            dma((12,)), dma((3,)),
            dma((4, 3)), dma((4, 3)),
            dma((4, 3)), dma((4, 3)),
            dma((SLICES + 1,)), dma((SLICES + 1,)),
            dma((2, 4)), dma((2, 4)),
            dma((8,)), dma((8,)),
            dma,
            pltpu.SemaphoreType.REGULAR,
            dma((SLICES, RUN)),
        ],
        compiler_params=pltpu.CompilerParams(
            collective_id=0, has_side_effects=True, vmem_limit_bytes=40 * 2**20
        ),
        cost_estimate=pl.CostEstimate(flops=1610612736, bytes_accessed=2**21, transcendentals=6144),
    )(*[pltpu.with_memory_space_constraint(operand, pltpu.HBM) for operand in operands])


def solution(mesh):
    placed = (P(("row", "col"), None), P(("row", "col"), None), P(), P(), P())
    return jax.shard_map(
        local, mesh=mesh, in_specs=placed, out_specs=P(None, "row", "col"), check_vma=False
    )
```

```python
import jax
import jax.numpy as jnp
from jax import lax
from jax.experimental import pallas as pl
from jax.experimental.pallas import tpu as pltpu
from jax.sharding import PartitionSpec as P

SLICES = 8
OCC_W = 256
VIR_W = 128
WIDTH = OCC_W + VIR_W
BLOCK = 16
ROWS = 256
COLS = 512
RUN = 4
NTAU = 2
MESH = pl.DeviceIdType.MESH


def gather_and_multiply(
    occ_hbm, vir_hbm, occ_energy_hbm, vir_energy_hbm, tau_hbm, out_ref,
    occ, vir, occ_energy, vir_energy, tau, own, scattered, lined, rows, cols, scales, total_occ, total_vir,
    in_sem, y_send, y_recv, x_send, x_recv, z_send, z_recv, up_send, up_recv, down_send, down_recv,
    pair_send, pair_recv, row_send, row_recv, core_send, core_recv, own_sem, go, straight_send, weighted_last,
):
    row, col = lax.axis_index("row"), lax.axis_index("col")
    y, z_lo = row // RUN, row % RUN
    x, z_hi, core = col // 4, col // 2 % 2, col % 2

    def at_y(steps):
        return ((row + RUN * steps) % (SLICES * RUN), col)

    def at_x(steps):
        return (row, (col + 4 * steps) % 16)

    over = col + 2 - 4 * z_hi
    across = (row, over)
    sibling = (row, col + 1 - 2 * core)
    pair = (y * RUN + z_lo + 1 - 2 * (z_lo % 2), col)

    parity, owner = z_lo % 2, z_lo // 2

    def spread(half, to):
        return (y * RUN + to, 4 * x + 2 * half + owner)

    def early_source(source_core):
        return (y * RUN + 2 * core + parity, 4 * x + source_core)

    def late_source(p, source_core):
        return (y * RUN + 2 * core + p, 4 * x + 2 + source_core)

    early, late = z_hi == 0, z_hi == 1

    inputs = [
        pltpu.make_async_copy(src, dst, in_sem.at[i])
        for i, (src, dst) in enumerate((
            (occ_hbm, occ), (vir_hbm, vir), (occ_energy_hbm, occ_energy), (vir_energy_hbm, vir_energy), (tau_hbm, tau),
        ))
    ]
    for copy in inputs:
        copy.start()

    barrier = pltpu.get_barrier_semaphore()
    lates = [late_source(p, c) for p in range(2) for c in range(2)]
    earlies = [early_source(c) for c in range(2)]
    partners = [at_y(s) for s in (4, 3, 5, 2, 6, 1, 7)] + [at_x(s) for s in (2, 1, 3)] + [pair, sibling]

    def signal(semaphore, places):
        for place in places:
            pl.semaphore_signal(semaphore, inc=1, device_id=place, device_id_type=MESH)

    signal(barrier, partners)

    straight = jnp.logical_and(late, y % 2 == 0)
    scatters = jnp.logical_or(early, y % 2 == 1)

    def straight_place(j, to):
        return (j * RUN + to, 4 * (y // 2) + owner)

    @pl.when(early)
    def _():
        signal(barrier, [across] + earlies + [spread(1, parity + 2 * i) for i in range(2)])
        signal(barrier, [(2 * x * RUN + 2 * core + p, 4 * there + 2 + c) for p in range(2) for there in range(4) for c in range(2)])

    @pl.when(late)
    def _():
        signal(barrier, lates)

    inputs[0].wait()
    inputs[1].wait()
    for j in range(SLICES):
        own[j, :, :OCC_W] = occ[:, j * OCC_W:(j + 1) * OCC_W]
        own[j, :, OCC_W:] = vir[:, j * VIR_W:(j + 1) * VIR_W]
    pl.semaphore_wait(barrier, len(partners) + 2 + 5 * z_hi + 32 * z_hi * (1 - y % 2))

    @pl.when(late)
    def _():
        signal(go, [across] + earlies)


    def remote(src, dst, send, recv, place):
        return pltpu.make_async_remote_copy(
            src_ref=src, dst_ref=dst, send_sem=send, recv_sem=recv, device_id=place, device_id_type=MESH
        )

    sent = []

    def launch(build, *args):
        sent.append((build, args))
        build(*args).start()

    def send(*args):
        launch(remote, *args)

    def arrived(ref, sem):
        pltpu.make_async_copy(ref, ref, sem).wait()

    def scatter_copy(steps):
        return remote(own.at[(y + steps) % SLICES], scattered.at[y], y_send.at[steps], y_recv, at_y(steps))

    around = (1, 7, 2, 6, 3, 5, 4)

    @pl.when(scatters)
    def _():
        for steps in around:
            scatter_copy(steps).start()
        pltpu.make_async_copy(own.at[y], scattered.at[y], y_recv).start()

    def straight_copy(j, to):
        spot = cols.at[j, parity, x, 1, pl.ds(pl.multiple_of(core * BLOCK, BLOCK), BLOCK)]
        return remote(own.at[j], spot, straight_send.at[j, to], z_recv.at[1 + parity], straight_place(j, to))

    @pl.when(straight)
    def _():
        for to in (0, 3, 1, 2):
            for j in range(SLICES):
                straight_copy(j, to).start()

    def row_spot(c):
        return rows.at[:, pl.ds(pl.multiple_of(c * BLOCK, BLOCK), BLOCK)]

    row_across = remote(own, row_spot(col), row_send.at[0, 0], row_recv.at[0, 0], across)
    sent.append((lambda: row_across, ()))

    @pl.when(late)
    def _():
        row_across.start()

    send(own, row_spot(col), core_send.at[0], core_recv.at[0], sibling)
    own_copy = pltpu.make_async_copy(own, row_spot(col), own_sem)
    own_copy.start()

    for i in range(2, 5):
        inputs[i].wait()
    for j in range(SLICES):
        for t in range(NTAU):
            tau_at = tau[:, t:t + 1]
            scales[j, t:t + 1, :OCC_W] = jnp.exp(tau_at * occ_energy[:, j * OCC_W:(j + 1) * OCC_W])
            scales[j, t:t + 1, OCC_W:] = jnp.exp(-tau_at * vir_energy[:, j * VIR_W:(j + 1) * VIR_W])

    def pair_of_planes(steps):
        there = (x + steps) % 4
        return scattered.at[pl.ds(2 * there, 2)], lined.at[:, x]

    def odd_plane(steps):
        there = (x + steps) % 4
        return scattered.at[2 * there + 1], lined.at[1, x]

    def exchange_copy(parts, steps):
        src, dst = parts(steps)
        return remote(src, dst, x_send.at[steps], x_recv, at_x(steps))

    def exchange(parts):
        for steps in (1, 3, 2):
            exchange_copy(parts, steps).start()
        src, dst = parts(0)
        pltpu.make_async_copy(src, dst, x_recv).start()

    @pl.when(early)
    def _():
        arrived(scattered, y_recv)
        exchange(pair_of_planes)
        arrived(lined, x_recv)

    @pl.when(late)
    def _():
        arrived(scattered.at[pl.ds(0, 4)], y_recv)
        exchange(odd_plane)
        arrived(lined.at[0], x_recv)

    spread_copies = []

    def spread_out(kind, half, to, active, slot):
        place = spread(half, to)
        spot = cols.at[y, parity, :, z_hi, pl.ds(pl.multiple_of(core * BLOCK, BLOCK), BLOCK)]
        here = jnp.logical_and(place[0] == row, place[1] == col)
        copy = remote(lined.at[half], spot, z_send.at[slot], z_recv.at[kind], place)
        there = jnp.logical_and(active, jnp.logical_not(here))
        spread_copies.append((there, copy))

        @pl.when(jnp.logical_and(active, here))
        def _():
            pltpu.make_async_copy(lined.at[half], spot, z_recv.at[kind]).start()

        @pl.when(there)
        def _():
            copy.start()

    for i in range(2):
        spread_out(0, 0, parity + 2 * i, early, i)
    for to in range(RUN):
        spread_out(1 + parity, 1, to, late, 4 + 2 * to + 1)

    def to_late_half():
        @pl.when(early)
        def _():
            pl.semaphore_wait(go, 3)

        for i in range(2):
            spread_out(0, 1, parity + 2 * i, early, 2 + i)

    def early_row_across():
        @pl.when(early)
        def _():
            row_across.start()

    def chunk(j, kind, xs=slice(0, 4)):
        p = (parity, 0, 1, 1 - parity)[kind]
        return cols.at[j, p, pl.ds(xs.start, xs.stop - xs.start), (0, 1, 1, 0)[kind]]

    whole, first, second = slice(0, 4), slice(0, 2), slice(2, 4)
    last_up = {0: first, 1: whole}
    last_down = {0: second, 2: whole}

    def up_copy(step, k, xs):
        ref = chunk((y + SLICES - step) % SLICES, k, xs)
        return remote(ref, ref, up_send.at[step, k], up_recv.at[step, k], at_y(1))

    def down_copy(step, k, xs):
        ref = chunk((y + step) % SLICES, k, xs)
        return remote(ref, ref, down_send.at[step, k], down_recv.at[step, k], at_y(7))

    def pair_copy(slot, xs):
        ref = chunk((y + (4 if slot == 8 else slot)) % SLICES, 0, xs)
        return remote(ref, ref, pair_send.at[slot], pair_recv.at[slot], pair)

    def pass_up(step, k, xs=whole):
        launch(up_copy, step, k, xs)

    def pass_down(step, k, xs=whole):
        launch(down_copy, step, k, xs)

    at_once = (z_lo % 3 == 0) == late

    def share(slot, xs=whole):
        @pl.when(at_once)
        def _():
            pair_copy(slot, xs).start()

    def share_later(slot, xs=whole):
        sent.append((pair_copy, (slot, xs)))

        @pl.when(jnp.logical_not(at_once))
        def _():
            pair_copy(slot, xs).start()

    def from_spread(k):
        arrived(chunk(y, k), z_recv.at[k])
        pass_up(0, k)
        pass_down(0, k)
        if k == 0:
            share(0)

    def from_below(step, k):
        xs = whole if step < 3 else last_up[k]
        j = (y + SLICES - step - 1) % SLICES
        arrived(chunk(j, k, xs), up_recv.at[step, k])
        if step < 2:
            pass_up(step + 1, k)
        elif step == 2 and k in last_up:
            pass_up(3, k, last_up[k])
        if k == 0:
            share(SLICES - step - 1, xs)

    def from_above(step, k):
        xs = whole if step < 3 else last_down[k]
        j = (y + step + 1) % SLICES
        arrived(chunk(j, k, xs), down_recv.at[step, k])
        if step < 2:
            pass_down(step + 1, k)
        elif step == 2 and k in last_down:
            pass_down(3, k, last_down[k])
        if k == 0:
            share(step + 1 if step < 3 else 8, xs)

    def from_both(step, k):
        from_below(step, k)
        from_above(step, k)

    def only(half, step, k):
        count = len(sent)

        @pl.when(half)
        def _():
            from_both(step, k)
        again = sent[count:]
        del sent[count:]
        return again

    contract = (((1,), (1,)), ((), ()))

    def weigh(j, t):
        panel = rows[j].astype(jnp.float32)
        return (panel * scales[j, pl.ds(t, 1), :]).astype(jnp.bfloat16)

    def grams(j, t, weighted=None):
        weighted = weigh(j, t) if weighted is None else weighted
        columns = cols[j].reshape(COLS, WIDTH)
        gram_occ = lax.dot_general(
            weighted[:, :OCC_W], columns[:, :OCC_W], contract, preferred_element_type=jnp.float32
        )
        gram_vir = lax.dot_general(
            weighted[:, OCC_W:], columns[:, OCC_W:], contract, preferred_element_type=jnp.float32
        )
        return gram_occ, gram_vir

    def accumulate(distance):
        j = (y + distance) % SLICES
        arrived(chunk(j, 3), pair_recv.at[distance])

        @pl.loop(0, NTAU)
        def _(t):
            gram_occ, gram_vir = grams(j, t)
            if distance == 0:
                total_occ[t] = gram_occ
                total_vir[t] = gram_vir
            else:
                total_occ[t] += gram_occ
                total_vir[t] += gram_vir

    def rows_from_across():
        arrived(row_spot(over), row_recv.at[0, 0])
        for steps in (1, 3, 2):
            send(row_spot(over), row_spot(over), row_send.at[1, steps], row_recv.at[1, steps], at_x(steps))
        send(row_spot(over), row_spot(over), core_send.at[1], core_recv.at[1], sibling)

    def rows_from_beside(which):
        for i, steps in enumerate((1, 3, 2)):
            c = ((over if which else col) + 16 - 4 * steps) % 16
            arrived(row_spot(c), row_recv.at[which, steps])
            slot = 2 + 3 * which + i
            send(row_spot(c), row_spot(c), core_send.at[slot], core_recv.at[slot], sibling)

    def rows_complete():
        own_copy.wait()
        for slot in range(8):
            arrived(row_spot(col), core_recv.at[slot])

    to_late_half()
    from_spread(0)
    from_both(0, 0)
    early_row_across()
    sent += only(early, 1, 0)
    from_spread(1)
    for steps in (1, 3, 2):
        send(own, row_spot(col), row_send.at[0, steps], row_recv.at[0, steps], at_x(steps))
    from_spread(2)
    for slot in (0, 1, 7):
        share_later(slot)
    rows_from_across()
    sent += only(early, 2, 0)
    only(late, 1, 0)
    share_later(2)
    share_later(6)
    rows_from_beside(0)
    from_both(0, 1)
    from_both(0, 2)
    only(late, 2, 0)
    share_later(3)
    share_later(5)
    rows_from_beside(1)
    from_both(1, 1)
    from_both(1, 2)
    rows_complete()
    for distance in (0, 1, 7):
        accumulate(distance)
    from_both(3, 0)
    share_later(4, first)
    share_later(8, second)
    from_both(2, 1)
    from_both(2, 2)
    for distance in (2, 6, 3, 5):
        accumulate(distance)
    last = (y + 4) % SLICES
    for t in range(NTAU):
        weighted_last[t] = weigh(last, t)
    from_below(3, 1)
    from_above(3, 2)
    arrived(chunk(last, 3, first), pair_recv.at[4])
    arrived(chunk(last, 3, second), pair_recv.at[8])
    for t in range(NTAU):
        gram_occ, gram_vir = grams(last, t, weighted_last[t])
        out_ref[t] = -((total_occ[t] + gram_occ) * (total_vir[t] + gram_vir))

    for build, args in sent:
        build(*args).wait_send()
    @pl.when(scatters)
    def _():
        for steps in around:
            scatter_copy(steps).wait_send()

    @pl.when(straight)
    def _():
        for j in range(SLICES):
            for to in range(RUN):
                straight_copy(j, to).wait_send()

    for steps in (1, 3, 2):
        @pl.when(early)
        def _():
            exchange_copy(pair_of_planes, steps).wait_send()

        @pl.when(late)
        def _():
            exchange_copy(odd_plane, steps).wait_send()

    for there, copy in spread_copies:
        @pl.when(there)
        def _():
            copy.wait_send()


def local(occ_orbitals, vir_orbitals, occ_energy, vir_energy, tau_points):
    dma = pltpu.SemaphoreType.DMA
    place = pl.BlockSpec(memory_space=pl.ANY)
    bf16, f32 = jnp.bfloat16, jnp.float32
    operands = (occ_orbitals, vir_orbitals, occ_energy.reshape(1, -1), vir_energy.reshape(1, -1), tau_points.reshape(1, -1))
    return pl.pallas_call(
        gather_and_multiply,
        out_shape=jax.ShapeDtypeStruct((NTAU, ROWS, COLS), f32),
        in_specs=[place] * 5,
        out_specs=pl.BlockSpec(memory_space=pltpu.VMEM),
        scratch_shapes=[
            pltpu.VMEM(occ_orbitals.shape, bf16),
            pltpu.VMEM(vir_orbitals.shape, bf16),
            pltpu.VMEM((1, SLICES * OCC_W), f32),
            pltpu.VMEM((1, SLICES * VIR_W), f32),
            pltpu.VMEM((1, NTAU), f32),
            pltpu.VMEM((SLICES, BLOCK, WIDTH), bf16),
            pltpu.VMEM((SLICES, BLOCK, WIDTH), bf16),
            pltpu.VMEM((2, 4, BLOCK, WIDTH), bf16),
            pltpu.VMEM((SLICES, ROWS, WIDTH), bf16),
            pltpu.VMEM((SLICES, 2, 4, 2, 2 * BLOCK, WIDTH), bf16),
            pltpu.VMEM((SLICES, NTAU, WIDTH), f32),
            pltpu.VMEM((NTAU, ROWS, COLS), f32),
            pltpu.VMEM((NTAU, ROWS, COLS), f32),
            dma((5,)),
            dma((SLICES,)), dma,
            dma((4,)), dma,
            dma((12,)), dma((3,)),
            dma((4, 3)), dma((4, 3)),
            dma((4, 3)), dma((4, 3)),
            dma((SLICES + 1,)), dma((SLICES + 1,)),
            dma((2, 4)), dma((2, 4)),
            dma((8,)), dma((8,)),
            dma,
            pltpu.SemaphoreType.REGULAR,
            dma((SLICES, RUN)),
            pltpu.VMEM((NTAU, ROWS, WIDTH), bf16),
        ],
        compiler_params=pltpu.CompilerParams(
            collective_id=0, has_side_effects=True, vmem_limit_bytes=40 * 2**20
        ),
        cost_estimate=pl.CostEstimate(flops=1610612736, bytes_accessed=2**21, transcendentals=6144),
    )(*[pltpu.with_memory_space_constraint(operand, pltpu.HBM) for operand in operands])


def solution(mesh):
    placed = (P(("row", "col"), None), P(("row", "col"), None), P(), P(), P())
    return jax.shard_map(
        local, mesh=mesh, in_specs=placed, out_specs=P(None, "row", "col"), check_vma=False
    )
```
